256 devices in a mesh: band: 8 (over z_hi, x), pw: 32 (over z_lo, y, core).
Axes of the slice: x: 4, y: 4, z: 8 (z_hi: 2, z_lo: 4; z = z_hi * 4 + z_lo), core: 2. Of those that a mesh axis runs over, the one named last changes fastest.
Arguments:
- orbitals: float32 [8, 2, 2, 192, 4096], P('band', None, None, None, 'pw'), may hold values from -6 to 6
- potential: float32 [192, 192, 192], P('pw'), may hold values from -2 to 2
- projectors: float32 [8, 2, 192, 4096], P(None, None, None, 'pw'), may hold values from -6 to 6
- coupling: float32 [8, 8], replicated, may hold values from -0.9 to 0.9
- columns: int32 [4096], P('pw'), may hold values from 0 to 36863, as said below
Outputs:
- applied: float32 [8, 2, 2, 192, 4096], P('band', None, None, None, 'pw')
- cross_terms: float32 [8, 4, 2, 2, 2], P('band')
The draws below stay inside these ranges and needn't reach their ends.
Inputs may be any that keep to these rules, and one draw needn't show every extreme that they name: Distinct grid columns.
All inputs are finite; a program needn't handle non-finite values.
Results may differ from the reference program's by a relative error of at most 0.0039.
Values may be sent and summed in bfloat16 or wider, within the bound.
No kernel may reach another device: no remote copies, remote signals or barrier semaphores. Data moves between devices by JAX's collectives and lax.ppermute only.
A program may use at most 192 MiB of HBM per device.

```python
import jax
import jax.numpy as jnp
from jax import lax

GRID = 192
BANDS = 2
PROJ = 8
COLS = 4096
BLOCKS = 8


def draw_columns(key, part):
    key = jax.random.fold_in(key, 7)
    first_key, order_key = jax.random.split(key)
    inner = jax.random.permutation(first_key, GRID * GRID - 2)[:COLS - 2] + 1
    chosen = jnp.concatenate([jnp.array([0, GRID * GRID - 1], jnp.int32), inner.astype(jnp.int32)])
    return chosen[jax.random.permutation(order_key, COLS)]


def block_levels(own_key, extent, cuts, smallest, high):
    factor_of = 1.0
    for dim, blocks in cuts:
        draws = jax.random.uniform(jax.random.fold_in(jax.random.fold_in(own_key, 6), dim), (blocks,), jnp.float32, smallest / len(cuts), high / len(cuts))
        factor_of = factor_of * jnp.repeat(jnp.exp(draws), extent[dim] // blocks).reshape((-1,) + (1,) * (len(extent) - 1 - dim))
    return factor_of


def normal_values(key, extent, width, limit, cuts=(), kind=jnp.bfloat16):
    loudness = block_levels(key, extent, cuts, -0.22, 0.18) if cuts else 1.0
    drawn = jax.random.normal(key, extent, jnp.float32) * width * loudness
    return jnp.minimum(jnp.maximum(drawn, -limit), limit).astype(kind)


def setup_inputs(seed: int = 0) -> dict:
    key_list = jax.random.split(jax.random.key(seed), 6)
    return {
        "orbitals": normal_values(key_list[0], (BLOCKS, BANDS, 2, GRID, COLS), 1.0, 6.0, ((0, 8), (4, 32)), jnp.float32),
        "potential": jnp.clip(jax.random.uniform(key_list[1], (GRID, GRID, GRID), jnp.float32, -2.0, 2.0) * block_levels(key_list[1], (GRID, GRID, GRID), ((0, 32),), -0.4, 0.0), -2.0, 2.0),
        "projectors": normal_values(key_list[2], (PROJ, 2, GRID, COLS), 1.0, 6.0, ((3, 32),), jnp.float32),
        "coupling": normal_values(key_list[3], (PROJ, PROJ), 0.15, 0.9, (), jnp.float32),
        "columns": draw_columns(jax.random.fold_in(key_list[5], 71), 0),
    }


HIGHEST = lax.Precision.HIGHEST

def wrapped(freqs):
    return jnp.where(freqs >= GRID // 2, freqs - GRID, freqs)

def reference(orbitals, potential, projectors, coupling, columns):
    scale = 1.0 / jnp.sqrt(jnp.float32(COLS * GRID))
    wave_x = wrapped(columns // GRID)
    wave_y = wrapped(columns % GRID)
    wave_z = wrapped(jnp.arange(GRID, dtype=jnp.int32))
    squared = wave_z[:, None] * wave_z[:, None] + (wave_x * wave_x + wave_y * wave_y)[None, :]
    kinetic = 4.0 / (GRID * GRID) * squared.astype(jnp.float32)
    beta = projectors[:, 0] + 1j * projectors[:, 1]
    coupling_sym = 0.5 * (coupling + coupling.T)
    pot_xyz = jnp.transpose(potential, (1, 2, 0))

    def apply_block(block):
        wave = block[:, 0] + 1j * block[:, 1]
        grid_real = jnp.zeros((BANDS, GRID * GRID, GRID), jnp.float32).at[:, columns, :].set(jnp.transpose(block[:, 0], (0, 2, 1)))
        grid_imag = jnp.zeros((BANDS, GRID * GRID, GRID), jnp.float32).at[:, columns, :].set(jnp.transpose(block[:, 1], (0, 2, 1)))
        grid = (grid_real + 1j * grid_imag).reshape(BANDS, GRID, GRID, GRID)
        field = jnp.fft.ifftn(grid, axes=(1, 2, 3), norm='ortho') * pot_xyz
        back = jnp.fft.fftn(field, axes=(1, 2, 3), norm='ortho').reshape(BANDS, GRID * GRID, GRID)[:, columns, :]
        local = jnp.transpose(back, (0, 2, 1))
        projected = jnp.einsum('jzc,bzc->bj', jnp.conj(beta), wave, precision=HIGHEST) * scale
        mixed = jnp.einsum('bj,jk->bk', projected, coupling_sym, precision=HIGHEST)
        nonlocal_term = jnp.einsum('bk,kzc->bzc', mixed, beta, precision=HIGHEST)
        total = local + kinetic * wave + nonlocal_term
        return jnp.stack([jnp.real(total), jnp.imag(total)], axis=1)
    applied = lax.map(apply_block, orbitals)
    low_orbitals = lax.optimization_barrier(orbitals.astype(jnp.bfloat16)).astype(jnp.float32)
    low_applied = lax.optimization_barrier(applied.astype(jnp.bfloat16)).astype(jnp.float32)
    padded = jnp.pad(low_orbitals, ((2, 2), (0, 0), (0, 0), (0, 0), (0, 0)))
    results = []
    for offset in (-2, -1, 1, 2):
        others = padded[2 + offset:2 + offset + BLOCKS]
        cross_real = jnp.einsum('bmtzc,bntzc->bmn', others, low_applied, precision=HIGHEST)
        cross_imag = jnp.einsum('bmzc,bnzc->bmn', others[:, :, 0], low_applied[:, :, 1], precision=HIGHEST) - jnp.einsum('bmzc,bnzc->bmn', others[:, :, 1], low_applied[:, :, 0], precision=HIGHEST)
        results.append(jnp.stack([cross_real, cross_imag], axis=1))
    cross_terms = jnp.stack(results, axis=1) * scale
    return (applied, cross_terms)
```

```python
from functools import partial
import math

import jax
import jax.numpy as jnp
import numpy as np
from jax import lax
from jax.experimental import pallas as pl
from jax.experimental.pallas import tpu as pltpu
from jax.sharding import PartitionSpec as P

GRID = 192
BANDS = 2
PROJ = 8
PW = 32
LOCAL = 128
COLS = PW * LOCAL
DEPTH = GRID // PW
ROWS = 16
GROUPS = 4
SPAN = GRID // GROUPS
LANES = 128
WIDTH = LANES // GROUPS
BF = jnp.bfloat16
F32 = jnp.float32
HIGHEST = lax.Precision.HIGHEST


def dft_tables():
    index = np.arange(GRID)
    angle = (index[:, None] * index[None, :] % GRID) * (2.0 * math.pi / GRID)
    factor = 1.0 / math.sqrt(GRID)
    return np.cos(angle) * factor, np.sin(angle) * factor


def build_tables():
    cos, sin = dft_tables()
    inverse = np.block([[cos, -sin], [sin, cos]])
    forward = np.block([[cos, sin], [-sin, cos]])
    place = np.zeros((PW, ROWS), np.int64) - 1
    for d in range(PW):
        for ri in range(2):
            for zi in range(DEPTH):
                place[d, ri * DEPTH + zi] = ri * GRID + d * DEPTH + zi
    flat = place.reshape(-1)
    to_planes = np.where((flat >= 0)[:, None], inverse[np.maximum(flat, 0)], 0.0)
    from_planes = np.where((flat >= 0)[None, :], forward[:, np.maximum(flat, 0)], 0.0)
    used = BANDS * 2 * DEPTH
    spread = np.zeros((8, 2 * LANES, 2 * LANES))
    for s in range(8):
        for b in range(BANDS):
            for r in range(2 * DEPTH):
                for g in range(GROUPS):
                    spread[s, b * LANES + s * ROWS + r, g * WIDTH + b * 2 * DEPTH + r] = 1.0
        spread[s, s * ROWS + 2 * DEPTH, LANES:] = 1.0
    turn = np.zeros((LANES, LANES))
    fold = np.zeros((2 * ROWS, LANES))
    for g in range(GROUPS):
        for b in range(BANDS):
            for zi in range(DEPTH):
                re = g * WIDTH + b * 2 * DEPTH + zi
                im = re + DEPTH
                turn[re, im] = -1.0
                turn[im, re] = 1.0
                fold[b * ROWS + zi, re] = 1.0
                fold[b * ROWS + DEPTH + zi, im] = 1.0
    unit = np.eye(LANES)
    return dict(
        to_planes=to_planes,
        from_planes=from_planes,
        spread=spread,
        y_table=np.concatenate([cos, sin], axis=0),
        mix_in=np.concatenate([unit, turn], axis=1),
        mix_out=np.concatenate([unit, turn], axis=0),
        x_inverse=inverse,
        x_forward=forward,
        fold=fold,
    )


def dot(a, b, precision=None):
    return lax.dot_general(
        a, b, (((1,), (0,)), ((), ())), precision=precision, preferred_element_type=F32
    )


def dot_nt(a, b, precision=None):
    return lax.dot_general(
        a, b, (((1,), (1,)), ((), ())), precision=precision, preferred_element_type=F32
    )


def wrapped(freqs):
    return jnp.where(freqs >= GRID // 2, freqs - GRID, freqs)


def send_kernel(block_ref, beta_ref, columns_ref, table_ref, send_ref):
    sums = []
    for b in range(BANDS):
        for j in range(PROJ):
            br, bi = beta_ref[j, 0], beta_ref[j, 1]
            wr, wi = block_ref[b, 0], block_ref[b, 1]
            sums.append(jnp.sum(br * wr + bi * wi, axis=0, keepdims=True))
            sums.append(jnp.sum(br * wi - bi * wr, axis=0, keepdims=True))
    stacked = jnp.concatenate(sums, axis=0)
    spread = jnp.concatenate([stacked, jnp.zeros((LANES - 32, LANES), F32)], axis=0)
    total = dot_nt(jnp.ones((8, LANES), F32), spread, HIGHEST)[0:1]
    high = total.astype(BF).astype(F32)
    middle = (total - high).astype(BF).astype(F32)
    low = total - high - middle
    cols = columns_ref[...]
    col_x = cols // GRID
    first = jnp.concatenate([col_x, cols - col_x * GRID], axis=1).astype(F32)
    other = jnp.concatenate([high, middle, low], axis=0)
    other = jnp.concatenate([other, jnp.zeros((3, LANES), F32)], axis=1)
    meta = jnp.concatenate([jnp.zeros((2 * DEPTH, 2 * LANES), F32), first, other], axis=0)
    wave = jnp.concatenate(
        [jnp.concatenate([block_ref[b, 0], block_ref[b, 1]], axis=0) for b in range(BANDS)], axis=1
    )
    lines = dot(table_ref[...], wave, HIGHEST)
    lines = lines.reshape(PW, ROWS, 2 * LANES) + meta[None]
    send_ref[...] = lines.astype(BF)


def planes_kernel(
    index_ref,
    recv_ref,
    pot_ref,
    spread_ref,
    y_ref,
    mix_in_ref,
    mix_out_ref,
    x_inv_ref,
    x_fwd_ref,
    fold_ref,
    back_ref,
    rows_ref,
    mask_ref,
    grid_ref,
    near_ref,
    far_ref,
):
    lane_group = lax.broadcasted_iota(jnp.int32, (1, LANES), 1) // WIDTH
    group_start = (lane_group * SPAN).astype(F32)
    turned = recv_ref[...].astype(F32).T.astype(BF)
    for s in range(8):
        for g in range(PW // 8):
            left = jnp.concatenate(
                [
                    turned[0:LANES, g * LANES : (g + 1) * LANES],
                    turned[LANES : 2 * LANES, g * LANES : (g + 1) * LANES],
                ],
                axis=1,
            )
            both = dot(left, spread_ref[s])
            start = (g * 8 + s) * LANES
            rows_ref[start : start + LANES, :] = both[:, :LANES]
            offset = both[:, LANES:] - group_start
            mask_ref[start : start + LANES, :] = jnp.where(
                (offset >= 0.0) & (offset < SPAN), 1.0, 0.0
            )

    def clear(i, _):
        grid_ref[pl.ds(pl.multiple_of(i * 256, 256), 256), :] = jnp.zeros((256, LANES), F32)
        return 0

    lax.fori_loop(0, SPAN * GRID // 256, clear, 0)

    def scatter(i, _):
        base = pl.multiple_of(i * 16, 16)
        for u in range(16):
            code = index_ref[base + u]
            row = rows_ref[pl.ds(base + u, 1), :]
            pltpu.store(
                grid_ref.at[pl.ds(code >> 2, 1), :], row, mask=lane_group == (code & 3)
            )
        return 0

    lax.fori_loop(0, COLS // 16, scatter, 0)

    def along_y_in(i, _):
        base = pl.multiple_of(i * 2 * GRID, 2 * GRID)
        pair = jnp.concatenate(
            [grid_ref[pl.ds(base, GRID), :], grid_ref[pl.ds(base + GRID, GRID), :]], axis=1
        ).astype(BF)
        both = dot(y_ref[...], pair).astype(BF)
        for h in range(2):
            part = jnp.concatenate(
                [
                    both[:GRID, h * LANES : (h + 1) * LANES],
                    both[GRID:, h * LANES : (h + 1) * LANES],
                ],
                axis=1,
            )
            mixed = dot_nt(mix_in_ref[...], part)
            place = pl.ds(pl.multiple_of((2 * i + h) * LANES, LANES), LANES)
            near_ref[place, :] = mixed[:, :LANES]
            far_ref[place, :] = jnp.concatenate(
                [mixed[:, LANES:], jnp.zeros((LANES, 2 * LANES - GRID), F32)], axis=1
            )
        return 0

    lax.fori_loop(0, SPAN // 2, along_y_in, 0)

    for b in range(BANDS):
        for zi in range(DEPTH):
            lane = b * 2 * DEPTH + zi
            places = [
                pl.ds(g * WIDTH + lane + ri * DEPTH, SPAN, stride=LANES)
                for ri in range(2)
                for g in range(GROUPS)
            ]
            plane = jnp.concatenate(
                [
                    jnp.concatenate([ref[place, :] for place in places], axis=0)
                    for ref in (near_ref, far_ref)
                ],
                axis=1,
            ).astype(BF)
            field = dot(x_inv_ref[...], plane)
            pot = jnp.concatenate(
                [pot_ref[zi], jnp.zeros((GRID, 2 * LANES - GRID), F32)], axis=1
            )
            field = (field * jnp.concatenate([pot, pot], axis=0)).astype(BF)
            back = dot(x_fwd_ref[...], field)
            for k, place in enumerate(places):
                near_ref[place, :] = back[k * SPAN : (k + 1) * SPAN, :LANES]
                far_ref[place, :] = back[k * SPAN : (k + 1) * SPAN, LANES:]

    def along_y_out(i, _):
        place = pl.ds(pl.multiple_of(i * 2 * LANES, 2 * LANES), 2 * LANES)
        pair = jnp.concatenate(
            [near_ref[place, :], far_ref[place, : GRID - LANES]], axis=1
        ).astype(BF)
        both = dot_nt(y_ref[...], pair).astype(BF)
        base = pl.multiple_of(i * 2 * GRID, 2 * GRID)
        for h in range(2):
            part = jnp.concatenate(
                [
                    both[:GRID, h * LANES : (h + 1) * LANES],
                    both[GRID:, h * LANES : (h + 1) * LANES],
                ],
                axis=1,
            )
            grid_ref[pl.ds(base + h * GRID, GRID), :] = dot(part, mix_out_ref[...])
        return 0

    lax.fori_loop(0, SPAN // 2, along_y_out, 0)

    def gather(i, _):
        base = pl.multiple_of(i * 16, 16)
        for u in range(16):
            code = index_ref[base + u]
            rows_ref[pl.ds(base + u, 1), :] = grid_ref[pl.ds(code >> 2, 1), :]
        return 0

    lax.fori_loop(0, COLS // 16, gather, 0)

    for d in range(PW):
        part = slice(d * LANES, (d + 1) * LANES)
        kept = (rows_ref[part, :] * mask_ref[part, :]).astype(BF)
        folded = dot_nt(fold_ref[...], kept).astype(BF)
        back_ref[d * ROWS : (d + 1) * ROWS, 0:LANES] = folded[:ROWS]
        back_ref[d * ROWS : (d + 1) * ROWS, LANES:] = folded[ROWS:]


def finish_kernel(
    mixed_ref, back_ref, block_ref, beta_ref, columns_ref, table_ref, *rest
):
    others = rest[:4]
    applied_ref, cross_ref, local_ref = rest[4:]
    local_ref[...] = dot(table_ref[0], back_ref[...]) + dot(table_ref[1], back_ref[...])
    cols = columns_ref[...]
    col_x = cols // GRID
    fx = wrapped(col_x)
    fy = wrapped(cols - col_x * GRID)
    fxy = fx * fx + fy * fy
    chunk = 48
    totals = [jnp.zeros((8, LANES), F32) for _ in range(32)]
    for start in range(0, GRID, chunk):
        part = slice(start, start + chunk)
        fz = wrapped(lax.broadcasted_iota(jnp.int32, (chunk, LANES), 0) + start)
        kinetic = (fz * fz + fxy).astype(F32) * (4.0 / (GRID * GRID))
        low = []
        for b in range(BANDS):
            real = local_ref[start : start + chunk, b * LANES : (b + 1) * LANES]
            imag = local_ref[GRID + start : GRID + start + chunk, b * LANES : (b + 1) * LANES]
            real = real + kinetic * block_ref[b, 0, part]
            imag = imag + kinetic * block_ref[b, 1, part]
            for k in range(PROJ):
                mr = mixed_ref[b * 2 * PROJ + 2 * k]
                mi = mixed_ref[b * 2 * PROJ + 2 * k + 1]
                br, bi = beta_ref[k, 0, part], beta_ref[k, 1, part]
                real = real + mr * br - mi * bi
                imag = imag + mr * bi + mi * br
            applied_ref[b, 0, part] = real
            applied_ref[b, 1, part] = imag
            low.append((real.astype(BF).astype(F32), imag.astype(BF).astype(F32)))
        for o in range(4):
            for m in range(BANDS):
                otr = others[o][m, 0, part].astype(F32)
                oti = others[o][m, 1, part].astype(F32)
                for n in range(BANDS):
                    ar, ai = low[n]
                    real = (otr * ar + oti * ai).reshape(chunk // 8, 8, LANES).sum(0)
                    imag = (otr * ai - oti * ar).reshape(chunk // 8, 8, LANES).sum(0)
                    totals[o * 8 + m * 2 + n] += real
                    totals[o * 8 + 4 + m * 2 + n] += imag
    stacked = jnp.concatenate([jnp.sum(t, axis=0, keepdims=True) for t in totals], axis=0)
    spread = jnp.concatenate([stacked, jnp.zeros((LANES - 32, LANES), F32)], axis=0)
    cross_ref[...] = dot_nt(jnp.ones((8, LANES), F32), spread, HIGHEST)


def from_behind(value, axis, steps):
    count = lax.axis_size(axis)
    first, last = max(0, -steps), min(count, count - steps)
    return lax.ppermute(value, axis, [(s, s + steps) for s in range(first, last)])


def vmem():
    return pl.BlockSpec(memory_space=pltpu.VMEM)


def smem():
    return pl.BlockSpec(memory_space=pltpu.SMEM)


def exchange(value):
    return lax.all_to_all(value, "pw", split_axis=0, concat_axis=0, tiled=True)


def per_device(orbitals, potential, projectors, coupling, columns):
    tables = build_tables()
    half = {k: jnp.asarray(v, BF) for k, v in tables.items()}
    block = orbitals[0]
    own_columns = columns.reshape(1, LOCAL)
    scale = 1.0 / math.sqrt(COLS * GRID)
    low_orbitals = block.astype(BF)
    others = [from_behind(low_orbitals, "band", -offset) for offset in (-2, -1, 1, 2)]

    sent = pl.pallas_call(
        send_kernel,
        name="lines_out",
        out_shape=jax.ShapeDtypeStruct((PW, ROWS, 2 * LANES), BF),
        in_specs=[vmem()] * 4,
        out_specs=vmem(),
        compiler_params=pltpu.CompilerParams(vmem_limit_bytes=32 << 20),
    )(block, projectors, own_columns, jnp.asarray(tables["to_planes"], F32))
    recv = exchange(sent)

    all_x = recv[:, 2 * DEPTH, :LOCAL].astype(jnp.int32)
    all_y = recv[:, 2 * DEPTH, LOCAL:].astype(jnp.int32)
    index = (((all_x % SPAN) * GRID + all_y) * GROUPS + all_x // SPAN).reshape(COLS)
    proj = jnp.sum(recv[:, 2 * DEPTH + 1 :, :32].astype(F32), axis=(0, 1))
    proj = proj.reshape(BANDS, PROJ, 2) * scale
    coupling_sym = 0.5 * (coupling + coupling.T)
    mixed = jnp.sum(proj[:, :, None, :] * coupling_sym[None, :, :, None], axis=1)
    mixed = mixed.reshape(BANDS * PROJ * 2)

    back = pl.pallas_call(
        planes_kernel,
        name="planes",
        out_shape=jax.ShapeDtypeStruct((PW * ROWS, 2 * LANES), BF),
        in_specs=[smem()] + [vmem()] * 9,
        out_specs=vmem(),
        scratch_shapes=[
            pltpu.VMEM((COLS, LANES), F32),
            pltpu.VMEM((COLS, LANES), F32),
            pltpu.VMEM((SPAN * GRID, LANES), F32),
            pltpu.VMEM((SPAN * LANES, LANES), F32),
            pltpu.VMEM((SPAN * LANES, LANES), F32),
        ],
        compiler_params=pltpu.CompilerParams(vmem_limit_bytes=48 << 20),
    )(
        index,
        recv.reshape(PW * ROWS, 2 * LANES),
        potential,
        half["spread"],
        half["y_table"],
        half["mix_in"],
        half["mix_out"],
        half["x_inverse"],
        half["x_forward"],
        half["fold"],
    )
    returned = exchange(back.reshape(PW, ROWS, 2 * LANES)).reshape(PW * ROWS, 2 * LANES)

    exact = tables["from_planes"]
    rounded = exact.astype(jnp.bfloat16).astype(np.float64)
    pair = jnp.asarray(np.stack([rounded, exact - rounded]), BF)
    applied, cross = pl.pallas_call(
        finish_kernel,
        name="lines_in",
        out_shape=(
            jax.ShapeDtypeStruct((BANDS, 2, GRID, LOCAL), F32),
            jax.ShapeDtypeStruct((8, LANES), F32),
        ),
        in_specs=[smem()] + [vmem()] * 9,
        out_specs=(vmem(), vmem()),
        scratch_shapes=[pltpu.VMEM((2 * GRID, 2 * LANES), F32)],
        compiler_params=pltpu.CompilerParams(vmem_limit_bytes=32 << 20),
    )(mixed, returned, block, projectors, own_columns, pair, *others)
    every = exchange(jnp.broadcast_to(cross[0:1], (PW, LANES)))
    summed = jnp.sum(every[:, :32], axis=0).reshape(4, 2, BANDS, BANDS)
    return applied[None], (summed * scale)[None]


def solution(mesh):
    return jax.shard_map(
        per_device,
        mesh=mesh,
        in_specs=(
            P("band", None, None, None, "pw"),
            P("pw", None, None),
            P(None, None, None, "pw"),
            P(),
            P("pw"),
        ),
        out_specs=(P("band", None, None, None, "pw"), P("band", None, None, None, None)),
        check_vma=False,
    )
```

```python
from functools import partial
import math

import jax
import jax.numpy as jnp
import numpy as np
from jax import lax
from jax.experimental import pallas as pl
from jax.experimental.pallas import tpu as pltpu
from jax.sharding import PartitionSpec as P

GRID = 192
BANDS = 2
PROJ = 8
PW = 32
LOCAL = 128
COLS = PW * LOCAL
DEPTH = GRID // PW
ROWS = 16
GROUPS = 4
SPAN = GRID // GROUPS
LANES = 128
WIDTH = LANES // GROUPS
STEP = LANES + 1
BF = jnp.bfloat16
F32 = jnp.float32
HIGHEST = lax.Precision.HIGHEST


def dft_tables():
    index = np.arange(GRID)
    angle = (index[:, None] * index[None, :] % GRID) * (2.0 * math.pi / GRID)
    factor = 1.0 / math.sqrt(GRID)
    return np.cos(angle) * factor, np.sin(angle) * factor


def build_tables():
    cos, sin = dft_tables()
    inverse = np.block([[cos, -sin], [sin, cos]])
    forward = np.block([[cos, sin], [-sin, cos]])
    place = np.zeros((PW, ROWS), np.int64) - 1
    for d in range(PW):
        for ri in range(2):
            for zi in range(DEPTH):
                place[d, ri * DEPTH + zi] = ri * GRID + d * DEPTH + zi
    flat = place.reshape(-1)
    to_planes = np.where((flat >= 0)[:, None], inverse[np.maximum(flat, 0)], 0.0)
    from_planes = np.where((flat >= 0)[None, :], forward[:, np.maximum(flat, 0)], 0.0)
    used = BANDS * 2 * DEPTH
    spread = np.zeros((8, 2 * LANES, 2 * LANES))
    for s in range(8):
        for b in range(BANDS):
            for r in range(2 * DEPTH):
                for g in range(GROUPS):
                    spread[s, b * LANES + s * ROWS + r, g * WIDTH + b * 2 * DEPTH + r] = 1.0
        spread[s, s * ROWS + 2 * DEPTH, LANES:] = 1.0
    mix_in = np.zeros((LANES, 2 * LANES))
    mix_out = np.zeros((2 * LANES, LANES))
    fold = np.zeros((2 * ROWS, LANES))
    for g in range(GROUPS):
        for b in range(BANDS):
            for zi in range(DEPTH):
                re = g * WIDTH + b * 2 * DEPTH + zi
                im = re + DEPTH
                for h in range(GROUPS):
                    other = h * WIDTH + b * 2 * DEPTH + zi
                    for part, factor in ((0, 1.0), (LANES, 1j)):
                        turn = 1j ** (g * h % 4) * factor
                        mix_in[re, part + other] = turn.real
                        mix_in[re, part + other + DEPTH] = -turn.imag
                        mix_in[im, part + other] = turn.imag
                        mix_in[im, part + other + DEPTH] = turn.real
                        turn = turn.conjugate()
                        mix_out[part + other, re] = turn.real
                        mix_out[part + other + DEPTH, re] = -turn.imag
                        mix_out[part + other, im] = turn.imag
                        mix_out[part + other + DEPTH, im] = turn.real
                fold[b * ROWS + zi, re] = 1.0
                fold[b * ROWS + DEPTH + zi, im] = 1.0
    x_inverse = np.zeros((GROUPS, 2 * SPAN, 2 * SPAN))
    x_forward = np.zeros((GROUPS, 2 * SPAN, 2 * SPAN))
    for g in range(GROUPS):
        c, s = cos[:SPAN, g::GROUPS], sin[:SPAN, g::GROUPS]
        x_inverse[g] = np.block([[c.T, -s.T], [s.T, c.T]])
        x_forward[g] = np.block([[c, s], [-s, c]])
    return dict(
        to_planes=to_planes,
        from_planes=from_planes,
        spread=spread,
        y_table=np.concatenate([cos, sin], axis=0),
        mix_in=mix_in,
        mix_out=mix_out,
        x_inverse=x_inverse,
        x_forward=x_forward,
        fold=fold,
    )


def dot(a, b, precision=None):
    return lax.dot_general(
        a, b, (((1,), (0,)), ((), ())), precision=precision, preferred_element_type=F32
    )


def dot_nt(a, b, precision=None):
    return lax.dot_general(
        a, b, (((1,), (1,)), ((), ())), precision=precision, preferred_element_type=F32
    )


def wrapped(freqs):
    return jnp.where(freqs >= GRID // 2, freqs - GRID, freqs)


def load(source, target, sem):
    copy = pltpu.make_async_copy(source, target, sem)
    copy.start()
    return copy


def send_kernel(
    block_hbm,
    beta_hbm,
    columns_ref,
    table_hbm,
    send_hbm,
    low_hbm,
    block_ref,
    beta_ref,
    table_ref,
    lines_ref,
    low_ref,
    sems,
):
    block_copy = load(block_hbm, block_ref, sems.at[0])
    table_copy = load(table_hbm, table_ref, sems.at[1])
    beta_copies = [load(beta_hbm.at[j], beta_ref.at[j], sems.at[2 + j]) for j in range(PROJ)]
    block_copy.wait()
    low_ref[...] = block_ref[...].astype(BF)
    low_copy = load(low_ref, low_hbm, sems.at[11])
    wave = jnp.concatenate(
        [jnp.concatenate([block_ref[b, 0], block_ref[b, 1]], axis=0) for b in range(BANDS)], axis=1
    )
    wave_high = wave.astype(BF)
    wave_low = (wave - wave_high.astype(F32)).astype(BF)
    table_copy.wait()
    lines = dot(table_ref[0], wave_high) + (dot(table_ref[1], wave_high) + dot(table_ref[0], wave_low))
    sums = [None] * (BANDS * PROJ * 2)
    for j in range(PROJ):
        beta_copies[j].wait()
        for b in range(BANDS):
            br, bi = beta_ref[j, 0], beta_ref[j, 1]
            wr, wi = block_ref[b, 0], block_ref[b, 1]
            at = (b * PROJ + j) * 2
            sums[at] = jnp.sum(br * wr + bi * wi, axis=0, keepdims=True)
            sums[at + 1] = jnp.sum(br * wi - bi * wr, axis=0, keepdims=True)
    stacked = jnp.concatenate(sums, axis=0)
    spread = jnp.concatenate([stacked, jnp.zeros((LANES - 32, LANES), F32)], axis=0)
    total = dot_nt(jnp.ones((8, LANES), F32), spread, HIGHEST)[0:1]
    high = total.astype(BF).astype(F32)
    middle = (total - high).astype(BF).astype(F32)
    low = total - high - middle
    cols = columns_ref[...]
    col_x = cols // GRID
    first = jnp.concatenate([col_x, cols - col_x * GRID], axis=1).astype(F32)
    other = jnp.concatenate([high, middle, low], axis=0)
    other = jnp.concatenate([other, jnp.zeros((3, LANES), F32)], axis=1)
    meta = jnp.concatenate([jnp.zeros((2 * DEPTH, 2 * LANES), F32), first, other], axis=0)
    lines = lines.reshape(PW, ROWS, 2 * LANES) + meta[None]
    lines_ref[...] = lines.astype(BF)
    load(lines_ref, send_hbm, sems.at[10]).wait()
    low_copy.wait()


def planes_kernel(
    recv_hbm,
    pot_hbm,
    spread_hbm,
    y_hbm,
    mix_in_hbm,
    mix_out_hbm,
    x_inv_hbm,
    x_fwd_hbm,
    fold_hbm,
    couple_ref,
    back_hbm,
    mixed_ref,
    recv_ref,
    pot_ref,
    spread_ref,
    y_ref,
    mix_in_ref,
    mix_out_ref,
    x_inv_ref,
    x_fwd_ref,
    fold_ref,
    back_ref,
    rows_ref,
    mask_ref,
    grid_ref,
    near_ref,
    far_ref,
    near_out_ref,
    far_out_ref,
    near_pot_ref,
    far_pot_ref,
    place_ref,
    index_ref,
    sems,
):
    pairs = (
        (recv_hbm, recv_ref),
        (spread_hbm, spread_ref),
        (y_hbm, y_ref),
        (mix_in_hbm, mix_in_ref),
        (x_inv_hbm, x_inv_ref),
        (x_fwd_hbm, x_fwd_ref),
        (mix_out_hbm, mix_out_ref),
        (fold_hbm, fold_ref),
        (pot_hbm, pot_ref),
    )
    copies = [load(a, b, sems.at[k]) for k, (a, b) in enumerate(pairs)]

    def clear(i, _):
        grid_ref[pl.ds(pl.multiple_of(i * 256, 256), 256), :] = jnp.zeros((256, LANES), F32)
        return 0

    lax.fori_loop(0, SPAN * GRID // 256, clear, 0)
    copies[0].wait()
    lane = lax.broadcasted_iota(jnp.int32, (1, LANES), 1)
    group_start = (lane // WIDTH * SPAN).astype(F32)
    source = lax.broadcasted_iota(jnp.int32, (PW, PW * ROWS), 0)
    entry = lax.broadcasted_iota(jnp.int32, (PW, PW * ROWS), 1)
    pick = (entry == source * ROWS + 2 * DEPTH).astype(F32).astype(BF)
    xy = dot(pick, recv_ref[...])
    x, y = xy[:, :LANES], xy[:, LANES:]
    for g in range(1, GROUPS):
        x = jnp.where(x >= SPAN, x - SPAN, x)
    place_ref[...] = (x * GRID + y).astype(jnp.int32)
    index_copy = load(place_ref, index_ref, sems.at[13])
    copies[1].wait()
    turned = recv_ref[...].astype(F32).T
    entry = lax.broadcasted_iota(jnp.int32, (32, PW * ROWS), 1)
    sums = jnp.where(entry % ROWS > 2 * DEPTH, turned[:32], 0.0)
    sums = jnp.sum(sums, axis=1, keepdims=True) + jnp.zeros((32, LANES), F32)
    mixed_ref[...] = dot(couple_ref[...], sums, HIGHEST)
    turned = turned.astype(BF)
    for s in range(8):
        for g in range(PW // 8):
            left = jnp.concatenate(
                [
                    turned[0:LANES, g * LANES : (g + 1) * LANES],
                    turned[LANES : 2 * LANES, g * LANES : (g + 1) * LANES],
                ],
                axis=1,
            )
            both = dot(left, spread_ref[s])
            start = (g * 8 + s) * LANES
            rows_ref[start : start + LANES, :] = both[:, :LANES]
            offset = both[:, LANES:] - group_start
            mask_ref[start : start + LANES, :] = jnp.where(
                (offset >= 0.0) & (offset < SPAN), 1.0, 0.0
            )

    index_copy.wait()

    def scatter(i, _):
        base = pl.multiple_of(i * LOCAL, LOCAL)
        for u in range(LOCAL):
            place = pl.ds(index_ref[i, u], 1)
            row = pl.ds(base + u, 1)
            pltpu.store(grid_ref.at[place, :], rows_ref[row, :], mask=mask_ref[row, :] > 0.5)
        return 0

    lax.fori_loop(0, PW, scatter, 0)
    for copy in copies[2:]:
        copy.wait()
    for zi in range(DEPTH):
        part = slice(zi * GRID, (zi + 1) * GRID)
        near_pot_ref[part, :] = pot_ref[zi, :, :LANES]
        far_pot_ref[part, :] = jnp.concatenate(
            [pot_ref[zi, :, LANES:], jnp.zeros((GRID, 2 * LANES - GRID), F32)], axis=1
        )

    def along_y_in(i, _):
        base = pl.multiple_of(i * 2 * GRID, 2 * GRID)
        pair = jnp.concatenate(
            [grid_ref[pl.ds(base, GRID), :], grid_ref[pl.ds(base + GRID, GRID), :]], axis=1
        ).astype(BF)
        both = dot(y_ref[...], pair).astype(BF)
        for h in range(2):
            part = jnp.concatenate(
                [
                    both[:GRID, h * LANES : (h + 1) * LANES],
                    both[GRID:, h * LANES : (h + 1) * LANES],
                ],
                axis=1,
            )
            mixed = dot_nt(mix_in_ref[...], part)
            place = pl.ds((2 * i + h) * STEP, LANES)
            near_ref[place, :] = mixed[:, :LANES]
            far_ref[place, :] = jnp.concatenate(
                [mixed[:, LANES:], jnp.zeros((LANES, 2 * LANES - GRID), F32)], axis=1
            )
        return 0

    lax.fori_loop(0, SPAN // 2, along_y_in, 0, unroll=True)

    for zi in range(DEPTH):
        for g in range(GROUPS):
            part = pl.ds(zi * GRID + g, SPAN, stride=GROUPS)
            pot = jnp.concatenate([near_pot_ref[part, :], far_pot_ref[part, :]], axis=1)
            pot = jnp.concatenate([pot, pot], axis=0)
            for b in range(BANDS):
                lane = g * WIDTH + b * 2 * DEPTH + zi
                places = [pl.ds(lane + ri * DEPTH, SPAN, stride=STEP) for ri in range(2)]
                plane = jnp.concatenate(
                    [
                        jnp.concatenate([ref[place, :] for place in places], axis=0)
                        for ref in (near_ref, far_ref)
                    ],
                    axis=1,
                ).astype(BF)
                field = (dot(x_inv_ref[g], plane) * pot).astype(BF)
                back = dot(x_fwd_ref[g], field)
                for ri, place in enumerate(places):
                    near_out_ref[place, :] = back[ri * SPAN : (ri + 1) * SPAN, :LANES]
                    far_out_ref[place, :] = back[ri * SPAN : (ri + 1) * SPAN, LANES:]

    def along_y_out(i, _):
        places = [pl.ds((2 * i + h) * STEP, LANES) for h in range(2)]
        pair = jnp.concatenate(
            [
                jnp.concatenate([near_out_ref[place, :] for place in places], axis=0),
                jnp.concatenate([far_out_ref[place, : GRID - LANES] for place in places], axis=0),
            ],
            axis=1,
        ).astype(BF)
        both = dot_nt(y_ref[...], pair).astype(BF)
        base = pl.multiple_of(i * 2 * GRID, 2 * GRID)
        for h in range(2):
            part = jnp.concatenate(
                [
                    both[:GRID, h * LANES : (h + 1) * LANES],
                    both[GRID:, h * LANES : (h + 1) * LANES],
                ],
                axis=1,
            )
            grid_ref[pl.ds(base + h * GRID, GRID), :] = dot(part, mix_out_ref[...])
        return 0

    lax.fori_loop(0, SPAN // 2, along_y_out, 0, unroll=True)

    def gather(i, _):
        base = pl.multiple_of(i * LOCAL, LOCAL)
        for u in range(LOCAL):
            rows_ref[pl.ds(base + u, 1), :] = grid_ref[pl.ds(index_ref[i, u], 1), :]
        return 0

    lax.fori_loop(0, PW, gather, 0)

    outs = []
    for d in range(PW):
        part = slice(d * LANES, (d + 1) * LANES)
        kept = (rows_ref[part, :] * mask_ref[part, :]).astype(BF)
        folded = dot_nt(fold_ref[...], kept).astype(BF)
        back_ref[d * ROWS : (d + 1) * ROWS, 0:LANES] = folded[:ROWS]
        back_ref[d * ROWS : (d + 1) * ROWS, LANES:] = folded[ROWS:]
        if d % 8 == 7:
            piece = pl.ds((d - 7) * ROWS, 8 * ROWS)
            outs.append(load(back_ref.at[piece], back_hbm.at[piece], sems.at[9 + d // 8]))
    for copy in outs:
        copy.wait()


def finish_kernel(
    back_hbm,
    table_hbm,
    block_hbm,
    beta_hbm,
    next_hbm,
    past_hbm,
    mixed_ref,
    columns_ref,
    applied_hbm,
    cross_ref,
    back_ref,
    table_ref,
    block_ref,
    beta_ref,
    next_ref,
    past_ref,
    local_ref,
    applied_ref,
    sems,
):
    pairs = (
        (back_hbm, back_ref),
        (table_hbm, table_ref),
        (block_hbm, block_ref),
        (beta_hbm, beta_ref),
        (next_hbm, next_ref),
        (past_hbm, past_ref),
    )
    copies = [load(a, b, sems.at[k]) for k, (a, b) in enumerate(pairs)]
    cols = columns_ref[...]
    col_x = cols // GRID
    fx = wrapped(col_x)
    fy = wrapped(cols - col_x * GRID)
    fxy = fx * fx + fy * fy
    copies[0].wait()
    copies[1].wait()
    local_ref[...] = dot(table_ref[0], back_ref[...]) + dot(table_ref[1], back_ref[...])
    for copy in copies[2:]:
        copy.wait()
    chunk = 48
    totals = [jnp.zeros((8, LANES), F32) for _ in range(16)]
    outs = []
    for start in range(0, GRID, chunk):
        part = slice(start, start + chunk)
        fz = wrapped(lax.broadcasted_iota(jnp.int32, (chunk, LANES), 0) + start)
        kinetic = (fz * fz + fxy).astype(F32) * (4.0 / (GRID * GRID))
        low = []
        for b in range(BANDS):
            real = local_ref[start : start + chunk, b * LANES : (b + 1) * LANES]
            imag = local_ref[GRID + start : GRID + start + chunk, b * LANES : (b + 1) * LANES]
            real = real + kinetic * block_ref[b, 0, part]
            imag = imag + kinetic * block_ref[b, 1, part]
            for k in range(PROJ):
                at = (b * PROJ + k) * 2
                mr, mi = mixed_ref[at : at + 1, :], mixed_ref[at + 1 : at + 2, :]
                br, bi = beta_ref[k, 0, part], beta_ref[k, 1, part]
                real = real + mr * br - mi * bi
                imag = imag + mr * bi + mi * br
            applied_ref[b, 0, part] = real
            applied_ref[b, 1, part] = imag
            low.append((real.astype(BF).astype(F32), imag.astype(BF).astype(F32)))
        outs.append(
            load(
                applied_ref.at[:, :, pl.ds(start, chunk)],
                applied_hbm.at[:, :, pl.ds(start, chunk)],
                sems.at[6 + start // chunk],
            )
        )
        for o, other in enumerate((next_ref, past_ref)):
            for m in range(BANDS):
                otr = other[m, 0, part].astype(F32)
                oti = other[m, 1, part].astype(F32)
                for n in range(BANDS):
                    ar, ai = low[n]
                    real = (otr * ar + oti * ai).reshape(chunk // 8, 8, LANES).sum(0)
                    imag = (otr * ai - oti * ar).reshape(chunk // 8, 8, LANES).sum(0)
                    totals[o * 8 + m * 2 + n] += real
                    totals[o * 8 + 4 + m * 2 + n] += imag
    stacked = jnp.concatenate([jnp.sum(t, axis=0, keepdims=True) for t in totals], axis=0)
    spread = jnp.concatenate([stacked, jnp.zeros((LANES - 16, LANES), F32)], axis=0)
    cross_ref[...] = dot_nt(jnp.ones((8 * PW, LANES), F32), spread, HIGHEST)
    for copy in outs:
        copy.wait()


def from_behind(value, axis, steps):
    count = lax.axis_size(axis)
    first, last = max(0, -steps), min(count, count - steps)
    return lax.ppermute(value, axis, [(s, s + steps) for s in range(first, last)])


def vmem():
    return pl.BlockSpec(memory_space=pltpu.VMEM)


def hbm():
    return pl.BlockSpec(memory_space=pltpu.HBM)


def smem():
    return pl.BlockSpec(memory_space=pltpu.SMEM)


def exchange(value):
    return lax.all_to_all(value, "pw", split_axis=0, concat_axis=0, tiled=True)


def planes_call(recv, potential, half, couple, name="planes"):
    return pl.pallas_call(
        planes_kernel,
        name=name,
        out_shape=(
            jax.ShapeDtypeStruct((PW * ROWS, 2 * LANES), BF),
            jax.ShapeDtypeStruct((32, LANES), F32),
        ),
        in_specs=[hbm()] * 9 + [vmem()],
        out_specs=(hbm(), vmem()),
        scratch_shapes=[
            pltpu.VMEM((PW * ROWS, 2 * LANES), BF),
            pltpu.VMEM((DEPTH, GRID, GRID), F32),
        ]
        + [
            pltpu.VMEM(half[k].shape, BF)
            for k in ("spread", "y_table", "mix_in", "mix_out", "x_inverse", "x_forward", "fold")
        ]
        + [
            pltpu.VMEM((PW * ROWS, 2 * LANES), BF),
            pltpu.VMEM((COLS, LANES), F32),
            pltpu.VMEM((COLS, LANES), F32),
            pltpu.VMEM((SPAN * GRID, LANES), F32),
            pltpu.VMEM((SPAN * STEP, LANES), F32),
            pltpu.VMEM((SPAN * STEP, LANES), F32),
            pltpu.VMEM((SPAN * STEP, LANES), F32),
            pltpu.VMEM((SPAN * STEP, LANES), F32),
            pltpu.VMEM((DEPTH * GRID, LANES), F32),
            pltpu.VMEM((DEPTH * GRID, LANES), F32),
            pltpu.VMEM((PW, LOCAL), jnp.int32),
            pltpu.SMEM((PW, LOCAL), jnp.int32),
            pltpu.SemaphoreType.DMA((14,)),
        ],
        compiler_params=pltpu.CompilerParams(vmem_limit_bytes=64 << 20),
        cost_estimate=pl.CostEstimate(
            flops=20_000_000_000, bytes_accessed=4 << 20, transcendentals=0
        ),
    )(
        recv,
        potential,
        half["spread"],
        half["y_table"],
        half["mix_in"],
        half["mix_out"],
        half["x_inverse"],
        half["x_forward"],
        half["fold"],
        couple,
    )


def two_parts(exact):
    high = np.asarray(exact).astype(jnp.bfloat16).astype(np.float64)
    return jnp.asarray(np.stack([high, exact - high]), BF)


def per_device(orbitals, potential, projectors, coupling, columns):
    tables = build_tables()
    half = {k: jnp.asarray(v, BF) for k, v in tables.items()}
    block = orbitals[0]
    own_columns = columns.reshape(1, LOCAL)
    scale = 1.0 / math.sqrt(COLS * GRID)
    coupling_sym = 0.5 * (coupling + coupling.T)
    couple = jnp.einsum(
        "bc,jk,rs->bkrcjs",
        jnp.eye(BANDS, dtype=F32),
        coupling_sym * scale,
        jnp.eye(2, dtype=F32),
        precision=HIGHEST,
    ).reshape(32, 32)

    sent, low_orbitals = pl.pallas_call(
        send_kernel,
        name="lines_out",
        out_shape=(
            jax.ShapeDtypeStruct((PW, ROWS, 2 * LANES), BF),
            jax.ShapeDtypeStruct((BANDS, 2, GRID, LOCAL), BF),
        ),
        in_specs=[hbm(), hbm(), vmem(), hbm()],
        out_specs=(hbm(), hbm()),
        scratch_shapes=[
            pltpu.VMEM((BANDS, 2, GRID, LOCAL), F32),
            pltpu.VMEM((PROJ, 2, GRID, LOCAL), F32),
            pltpu.VMEM((2, PW * ROWS, 2 * GRID), BF),
            pltpu.VMEM((PW, ROWS, 2 * LANES), BF),
            pltpu.VMEM((BANDS, 2, GRID, LOCAL), BF),
            pltpu.SemaphoreType.DMA((12,)),
        ],
        compiler_params=pltpu.CompilerParams(vmem_limit_bytes=64 << 20),
    )(block, projectors, own_columns, two_parts(tables["to_planes"]))
    recv = exchange(sent)
    recv, low_orbitals = lax.optimization_barrier((recv, low_orbitals))
    following = from_behind(low_orbitals, "band", -1)
    preceding = from_behind(low_orbitals, "band", 2)

    back, mixed = planes_call(recv.reshape(PW * ROWS, 2 * LANES), potential, half, couple)
    returned = exchange(back.reshape(PW, ROWS, 2 * LANES)).reshape(PW * ROWS, 2 * LANES)

    applied, cross = pl.pallas_call(
        finish_kernel,
        name="lines_in",
        out_shape=(
            jax.ShapeDtypeStruct((BANDS, 2, GRID, LOCAL), F32),
            jax.ShapeDtypeStruct((8 * PW, LANES), F32),
        ),
        in_specs=[hbm()] * 6 + [vmem()] * 2,
        out_specs=(hbm(), vmem()),
        scratch_shapes=[
            pltpu.VMEM((PW * ROWS, 2 * LANES), BF),
            pltpu.VMEM((2, 2 * GRID, PW * ROWS), BF),
            pltpu.VMEM((BANDS, 2, GRID, LOCAL), F32),
            pltpu.VMEM((PROJ, 2, GRID, LOCAL), F32),
            pltpu.VMEM((BANDS, 2, GRID, LOCAL), BF),
            pltpu.VMEM((BANDS, 2, GRID, LOCAL), BF),
            pltpu.VMEM((2 * GRID, 2 * LANES), F32),
            pltpu.VMEM((BANDS, 2, GRID, LOCAL), F32),
            pltpu.SemaphoreType.DMA((10,)),
        ],
        compiler_params=pltpu.CompilerParams(vmem_limit_bytes=64 << 20),
    )(
        returned,
        two_parts(tables["from_planes"]),
        block,
        projectors,
        following,
        preceding,
        mixed,
        own_columns,
    )
    every = lax.all_to_all(cross, ("band", "pw"), split_axis=0, concat_axis=0, tiled=True)
    blocks = lax.axis_size("band")
    sums = jnp.sum(every[:, :16].reshape(blocks, PW, 16), axis=1) * scale
    rows = lax.axis_index("band") + jnp.asarray([0, -1, 0, 2], jnp.int32)
    picked = jnp.where(
        (rows[:, None] == jnp.arange(blocks)[None, :])[:, :, None], sums[None], 0.0
    ).sum(1)
    picked = picked.reshape(4, 2, 2, BANDS, BANDS)
    sign = jnp.asarray([1.0, -1.0], F32).reshape(2, 1, 1)
    adjoint = lambda v: jnp.swapaxes(v, 1, 2) * sign
    cross_terms = jnp.stack(
        [picked[2, 1], adjoint(picked[1, 0]), picked[0, 0], adjoint(picked[3, 1])]
    )
    return applied[None], cross_terms[None]


def solution(mesh):
    return jax.shard_map(
        per_device,
        mesh=mesh,
        in_specs=(
            P("band", None, None, None, "pw"),
            P("pw", None, None),
            P(None, None, None, "pw"),
            P(),
            P("pw"),
        ),
        out_specs=(P("band", None, None, None, "pw"), P("band", None, None, None, None)),
        check_vma=False,
    )
```

```python
from functools import partial
import math

import jax
import jax.numpy as jnp
import numpy as np
from jax import lax
from jax.experimental import pallas as pl
from jax.experimental.pallas import tpu as pltpu
from jax.sharding import PartitionSpec as P

GRID = 192
BANDS = 2
PROJ = 8
PW = 32
LOCAL = 128
COLS = PW * LOCAL
DEPTH = GRID // PW
ROWS = 16
GROUPS = 4
SPAN = GRID // GROUPS
LANES = 128
WIDTH = LANES // GROUPS
STEP = LANES + 1
BF = jnp.bfloat16
F32 = jnp.float32
HIGHEST = lax.Precision.HIGHEST


def dft_tables():
    index = np.arange(GRID)
    angle = (index[:, None] * index[None, :] % GRID) * (2.0 * math.pi / GRID)
    factor = 1.0 / math.sqrt(GRID)
    return np.cos(angle) * factor, np.sin(angle) * factor


def build_tables():
    cos, sin = dft_tables()
    inverse = np.block([[cos, -sin], [sin, cos]])
    forward = np.block([[cos, sin], [-sin, cos]])
    place = np.zeros((PW, ROWS), np.int64) - 1
    for d in range(PW):
        for ri in range(2):
            for zi in range(DEPTH):
                place[d, ri * DEPTH + zi] = ri * GRID + d * DEPTH + zi
    flat = place.reshape(-1)
    to_planes = np.where((flat >= 0)[:, None], inverse[np.maximum(flat, 0)], 0.0)
    from_planes = np.where((flat >= 0)[None, :], forward[:, np.maximum(flat, 0)], 0.0)
    used = BANDS * 2 * DEPTH
    spread = np.zeros((8, 2 * LANES, 2 * LANES))
    for s in range(8):
        for b in range(BANDS):
            for r in range(2 * DEPTH):
                for g in range(GROUPS):
                    spread[s, b * LANES + s * ROWS + r, g * WIDTH + b * 2 * DEPTH + r] = 1.0
        spread[s, s * ROWS + 2 * DEPTH, LANES:] = 1.0
    mix_in = np.zeros((LANES, 2 * LANES))
    mix_out = np.zeros((2 * LANES, LANES))
    fold = np.zeros((2 * ROWS, LANES))
    for g in range(GROUPS):
        for b in range(BANDS):
            for zi in range(DEPTH):
                re = g * WIDTH + b * 2 * DEPTH + zi
                im = re + DEPTH
                for h in range(GROUPS):
                    other = h * WIDTH + b * 2 * DEPTH + zi
                    for part, factor in ((0, 1.0), (LANES, 1j)):
                        turn = 1j ** (g * h % 4) * factor
                        mix_in[re, part + other] = turn.real
                        mix_in[re, part + other + DEPTH] = -turn.imag
                        mix_in[im, part + other] = turn.imag
                        mix_in[im, part + other + DEPTH] = turn.real
                        turn = turn.conjugate()
                        mix_out[part + other, re] = turn.real
                        mix_out[part + other + DEPTH, re] = -turn.imag
                        mix_out[part + other, im] = turn.imag
                        mix_out[part + other + DEPTH, im] = turn.real
                fold[b * ROWS + zi, re] = 1.0
                fold[b * ROWS + DEPTH + zi, im] = 1.0
    x_inverse = np.zeros((GROUPS, 2 * SPAN, 2 * SPAN))
    x_forward = np.zeros((GROUPS, 2 * SPAN, 2 * SPAN))
    for g in range(GROUPS):
        c, s = cos[:SPAN, g::GROUPS], sin[:SPAN, g::GROUPS]
        x_inverse[g] = np.block([[c.T, -s.T], [s.T, c.T]])
        x_forward[g] = np.block([[c, s], [-s, c]])
    return dict(
        to_planes=to_planes,
        from_planes=from_planes,
        spread=spread,
        y_table=np.concatenate([cos, sin], axis=0),
        mix_in=mix_in,
        mix_out=mix_out,
        x_inverse=x_inverse,
        x_forward=x_forward,
        fold=fold,
    )


def dot(a, b, precision=None):
    return lax.dot_general(
        a, b, (((1,), (0,)), ((), ())), precision=precision, preferred_element_type=F32
    )


def dot_nt(a, b, precision=None):
    return lax.dot_general(
        a, b, (((1,), (1,)), ((), ())), precision=precision, preferred_element_type=F32
    )


def wrapped(freqs):
    return jnp.where(freqs >= GRID // 2, freqs - GRID, freqs)


def load(source, target, sem):
    copy = pltpu.make_async_copy(source, target, sem)
    copy.start()
    return copy


def send_kernel(
    block_hbm,
    beta_hbm,
    columns_ref,
    table_hbm,
    send_hbm,
    low_hbm,
    block_ref,
    beta_ref,
    table_ref,
    lines_ref,
    low_ref,
    sems,
):
    block_copy = load(block_hbm, block_ref, sems.at[0])
    table_copy = load(table_hbm, table_ref, sems.at[1])
    beta_copies = [load(beta_hbm.at[j], beta_ref.at[j], sems.at[2 + j]) for j in range(PROJ)]
    block_copy.wait()
    low_ref[...] = block_ref[...].astype(BF)
    low_copy = load(low_ref, low_hbm, sems.at[11])
    wave = jnp.concatenate(
        [jnp.concatenate([block_ref[b, 0], block_ref[b, 1]], axis=0) for b in range(BANDS)], axis=1
    )
    wave_high = wave.astype(BF)
    wave_low = (wave - wave_high.astype(F32)).astype(BF)
    table_copy.wait()
    lines = dot(table_ref[0], wave_high) + (dot(table_ref[1], wave_high) + dot(table_ref[0], wave_low))
    sums = [None] * (BANDS * PROJ * 2)
    for j in range(PROJ):
        beta_copies[j].wait()
        for b in range(BANDS):
            br, bi = beta_ref[j, 0], beta_ref[j, 1]
            wr, wi = block_ref[b, 0], block_ref[b, 1]
            at = (b * PROJ + j) * 2
            sums[at] = jnp.sum(br * wr + bi * wi, axis=0, keepdims=True)
            sums[at + 1] = jnp.sum(br * wi - bi * wr, axis=0, keepdims=True)
    stacked = jnp.concatenate(sums, axis=0)
    spread = jnp.concatenate([stacked, jnp.zeros((LANES - 32, LANES), F32)], axis=0)
    total = dot_nt(jnp.ones((8, LANES), F32), spread, HIGHEST)[0:1]
    high = total.astype(BF).astype(F32)
    middle = (total - high).astype(BF).astype(F32)
    low = total - high - middle
    cols = columns_ref[...]
    col_x = cols // GRID
    first = jnp.concatenate([col_x, cols - col_x * GRID], axis=1).astype(F32)
    other = jnp.concatenate([high, middle, low], axis=0)
    other = jnp.concatenate([other, jnp.zeros((3, LANES), F32)], axis=1)
    meta = jnp.concatenate([jnp.zeros((2 * DEPTH, 2 * LANES), F32), first, other], axis=0)
    lines = lines.reshape(PW, ROWS, 2 * LANES) + meta[None]
    lines_ref[...] = lines.astype(BF)
    load(lines_ref, send_hbm, sems.at[10]).wait()
    low_copy.wait()


def planes_kernel(
    recv_hbm,
    pot_hbm,
    spread_hbm,
    y_hbm,
    mix_in_hbm,
    mix_out_hbm,
    x_inv_hbm,
    x_fwd_hbm,
    fold_hbm,
    coupling_ref,
    back_hbm,
    mixed_ref,
    recv_ref,
    pot_ref,
    spread_ref,
    y_ref,
    mix_in_ref,
    mix_out_ref,
    x_inv_ref,
    x_fwd_ref,
    fold_ref,
    back_ref,
    rows_ref,
    mask_ref,
    grid_ref,
    near_ref,
    far_ref,
    near_out_ref,
    far_out_ref,
    near_pot_ref,
    far_pot_ref,
    place_ref,
    index_ref,
    sems,
):
    pairs = (
        (recv_hbm, recv_ref),
        (spread_hbm, spread_ref),
        (y_hbm, y_ref),
        (mix_in_hbm, mix_in_ref),
        (x_inv_hbm, x_inv_ref),
        (x_fwd_hbm, x_fwd_ref),
        (mix_out_hbm, mix_out_ref),
        (fold_hbm, fold_ref),
        (pot_hbm, pot_ref),
    )
    copies = [load(a, b, sems.at[k]) for k, (a, b) in enumerate(pairs)]

    def clear(i, _):
        grid_ref[pl.ds(pl.multiple_of(i * 256, 256), 256), :] = jnp.zeros((256, LANES), F32)
        return 0

    lax.fori_loop(0, SPAN * GRID // 256, clear, 0)
    copies[0].wait()
    lane = lax.broadcasted_iota(jnp.int32, (1, LANES), 1)
    group_start = (lane // WIDTH * SPAN).astype(F32)
    source = lax.broadcasted_iota(jnp.int32, (PW, PW * ROWS), 0)
    entry = lax.broadcasted_iota(jnp.int32, (PW, PW * ROWS), 1)
    pick = (entry == source * ROWS + 2 * DEPTH).astype(F32).astype(BF)
    xy = dot(pick, recv_ref[...])
    x, y = xy[:, :LANES], xy[:, LANES:]
    for g in range(1, GROUPS):
        x = jnp.where(x >= SPAN, x - SPAN, x)
    place_ref[...] = (x * GRID + y).astype(jnp.int32)
    index_copy = load(place_ref, index_ref, sems.at[13])
    copies[1].wait()
    turned = recv_ref[...].astype(F32).T
    entry = lax.broadcasted_iota(jnp.int32, (32, PW * ROWS), 1)
    sums = jnp.where(entry % ROWS > 2 * DEPTH, turned[:32], 0.0)
    sums = jnp.sum(sums, axis=1, keepdims=True) + jnp.zeros((32, LANES), F32)
    row = lax.broadcasted_iota(jnp.int32, (32, 32), 0)
    column = lax.broadcasted_iota(jnp.int32, (32, 32), 1)
    same = (row // (2 * PROJ) == column // (2 * PROJ)) & (row % 2 == column % 2)
    row = lax.broadcasted_iota(jnp.int32, (32, PROJ), 0)
    column = lax.broadcasted_iota(jnp.int32, (32, PROJ), 1)
    widen = (row // 2 % PROJ == column).astype(F32)
    coupling = coupling_ref[...]
    couple = dot_nt(dot(widen, 0.5 * (coupling + coupling.T), HIGHEST), widen, HIGHEST)
    couple = jnp.where(same, couple * (1.0 / math.sqrt(COLS * GRID)), 0.0)
    mixed_ref[...] = dot(couple, sums, HIGHEST)
    turned = turned.astype(BF)
    for s in range(8):
        for g in range(PW // 8):
            left = jnp.concatenate(
                [
                    turned[0:LANES, g * LANES : (g + 1) * LANES],
                    turned[LANES : 2 * LANES, g * LANES : (g + 1) * LANES],
                ],
                axis=1,
            )
            both = dot(left, spread_ref[s])
            start = (g * 8 + s) * LANES
            rows_ref[start : start + LANES, :] = both[:, :LANES]
            offset = both[:, LANES:] - group_start
            mask_ref[start : start + LANES, :] = jnp.where(
                (offset >= 0.0) & (offset < SPAN), 1.0, 0.0
            )

    index_copy.wait()

    def scatter(i, _):
        base = pl.multiple_of(i * LOCAL, LOCAL)
        for u in range(LOCAL):
            place = pl.ds(index_ref[i, u], 1)
            row = pl.ds(base + u, 1)
            pltpu.store(grid_ref.at[place, :], rows_ref[row, :], mask=mask_ref[row, :] > 0.5)
        return 0

    lax.fori_loop(0, PW, scatter, 0)
    for copy in copies[2:]:
        copy.wait()
    for zi in range(DEPTH):
        part = slice(zi * GRID, (zi + 1) * GRID)
        near_pot_ref[part, :] = pot_ref[zi, :, :LANES]
        far_pot_ref[part, :] = jnp.concatenate(
            [pot_ref[zi, :, LANES:], jnp.zeros((GRID, 2 * LANES - GRID), F32)], axis=1
        )

    def along_y_in(i, _):
        base = pl.multiple_of(i * 2 * GRID, 2 * GRID)
        pair = jnp.concatenate(
            [grid_ref[pl.ds(base, GRID), :], grid_ref[pl.ds(base + GRID, GRID), :]], axis=1
        ).astype(BF)
        both = dot(y_ref[...], pair).astype(BF)
        for h in range(2):
            part = jnp.concatenate(
                [
                    both[:GRID, h * LANES : (h + 1) * LANES],
                    both[GRID:, h * LANES : (h + 1) * LANES],
                ],
                axis=1,
            )
            mixed = dot_nt(mix_in_ref[...], part)
            place = pl.ds((2 * i + h) * STEP, LANES)
            near_ref[place, :] = mixed[:, :LANES]
            far_ref[place, :] = jnp.concatenate(
                [mixed[:, LANES:], jnp.zeros((LANES, 2 * LANES - GRID), F32)], axis=1
            )
        return 0

    lax.fori_loop(0, SPAN // 2, along_y_in, 0, unroll=True)

    for zi in range(DEPTH):
        for g in range(GROUPS):
            part = pl.ds(zi * GRID + g, SPAN, stride=GROUPS)
            pot = jnp.concatenate([near_pot_ref[part, :], far_pot_ref[part, :]], axis=1)
            pot = jnp.concatenate([pot, pot], axis=0)
            for b in range(BANDS):
                lane = g * WIDTH + b * 2 * DEPTH + zi
                places = [pl.ds(lane + ri * DEPTH, SPAN, stride=STEP) for ri in range(2)]
                plane = jnp.concatenate(
                    [
                        jnp.concatenate([ref[place, :] for place in places], axis=0)
                        for ref in (near_ref, far_ref)
                    ],
                    axis=1,
                ).astype(BF)
                field = (dot(x_inv_ref[g], plane) * pot).astype(BF)
                back = dot(x_fwd_ref[g], field)
                for ri, place in enumerate(places):
                    near_out_ref[place, :] = back[ri * SPAN : (ri + 1) * SPAN, :LANES]
                    far_out_ref[place, :] = back[ri * SPAN : (ri + 1) * SPAN, LANES:]

    def along_y_out(i, _):
        places = [pl.ds((2 * i + h) * STEP, LANES) for h in range(2)]
        pair = jnp.concatenate(
            [
                jnp.concatenate([near_out_ref[place, :] for place in places], axis=0),
                jnp.concatenate([far_out_ref[place, : GRID - LANES] for place in places], axis=0),
            ],
            axis=1,
        ).astype(BF)
        both = dot_nt(y_ref[...], pair).astype(BF)
        base = pl.multiple_of(i * 2 * GRID, 2 * GRID)
        for h in range(2):
            part = jnp.concatenate(
                [
                    both[:GRID, h * LANES : (h + 1) * LANES],
                    both[GRID:, h * LANES : (h + 1) * LANES],
                ],
                axis=1,
            )
            grid_ref[pl.ds(base + h * GRID, GRID), :] = dot(part, mix_out_ref[...])
        return 0

    lax.fori_loop(0, SPAN // 2, along_y_out, 0, unroll=True)

    def gather(i, _):
        base = pl.multiple_of(i * LOCAL, LOCAL)
        for u in range(LOCAL):
            rows_ref[pl.ds(base + u, 1), :] = grid_ref[pl.ds(index_ref[i, u], 1), :]
        return 0

    lax.fori_loop(0, PW, gather, 0)

    outs = []
    for d in range(PW):
        part = slice(d * LANES, (d + 1) * LANES)
        kept = (rows_ref[part, :] * mask_ref[part, :]).astype(BF)
        folded = dot_nt(fold_ref[...], kept).astype(BF)
        back_ref[d * ROWS : (d + 1) * ROWS, 0:LANES] = folded[:ROWS]
        back_ref[d * ROWS : (d + 1) * ROWS, LANES:] = folded[ROWS:]
        if d % 8 == 7:
            piece = pl.ds((d - 7) * ROWS, 8 * ROWS)
            outs.append(load(back_ref.at[piece], back_hbm.at[piece], sems.at[9 + d // 8]))
    for copy in outs:
        copy.wait()


def finish_kernel(
    back_hbm,
    table_hbm,
    block_hbm,
    beta_hbm,
    mixed_ref,
    columns_ref,
    other_0,
    other_1,
    other_2,
    other_3,
    applied_hbm,
    cross_ref,
    back_ref,
    table_ref,
    block_ref,
    beta_ref,
    others_ref,
    local_ref,
    applied_ref,
    sems,
):
    pairs = (
        (back_hbm, back_ref),
        (table_hbm, table_ref),
        (block_hbm, block_ref),
        (beta_hbm, beta_ref),
        (other_0, others_ref.at[0]),
        (other_1, others_ref.at[1]),
        (other_2, others_ref.at[2]),
        (other_3, others_ref.at[3]),
    )
    copies = [load(a, b, sems.at[k]) for k, (a, b) in enumerate(pairs)]
    cols = columns_ref[...]
    col_x = cols // GRID
    fx = wrapped(col_x)
    fy = wrapped(cols - col_x * GRID)
    fxy = fx * fx + fy * fy
    copies[0].wait()
    copies[1].wait()
    local_ref[...] = dot(table_ref[0], back_ref[...]) + dot(table_ref[1], back_ref[...])
    for copy in copies[2:]:
        copy.wait()
    chunk = 48
    totals = [jnp.zeros((8, LANES), F32) for _ in range(32)]
    outs = []
    for start in range(0, GRID, chunk):
        part = slice(start, start + chunk)
        fz = wrapped(lax.broadcasted_iota(jnp.int32, (chunk, LANES), 0) + start)
        kinetic = (fz * fz + fxy).astype(F32) * (4.0 / (GRID * GRID))
        low = []
        for b in range(BANDS):
            real = local_ref[start : start + chunk, b * LANES : (b + 1) * LANES]
            imag = local_ref[GRID + start : GRID + start + chunk, b * LANES : (b + 1) * LANES]
            real = real + kinetic * block_ref[b, 0, part]
            imag = imag + kinetic * block_ref[b, 1, part]
            for k in range(PROJ):
                at = (b * PROJ + k) * 2
                mr, mi = mixed_ref[at : at + 1, :], mixed_ref[at + 1 : at + 2, :]
                br, bi = beta_ref[k, 0, part], beta_ref[k, 1, part]
                real = real + mr * br - mi * bi
                imag = imag + mr * bi + mi * br
            applied_ref[b, 0, part] = real
            applied_ref[b, 1, part] = imag
            low.append((real.astype(BF).astype(F32), imag.astype(BF).astype(F32)))
        outs.append(
            load(
                applied_ref.at[:, :, pl.ds(start, chunk)],
                applied_hbm.at[:, :, pl.ds(start, chunk)],
                sems.at[8 + start // chunk],
            )
        )
        for o in range(4):
            for m in range(BANDS):
                otr = others_ref[o, m, 0, part].astype(F32)
                oti = others_ref[o, m, 1, part].astype(F32)
                for n in range(BANDS):
                    ar, ai = low[n]
                    real = (otr * ar + oti * ai).reshape(chunk // 8, 8, LANES).sum(0)
                    imag = (otr * ai - oti * ar).reshape(chunk // 8, 8, LANES).sum(0)
                    totals[o * 8 + m * 2 + n] += real
                    totals[o * 8 + 4 + m * 2 + n] += imag
    stacked = jnp.concatenate([jnp.sum(t, axis=0, keepdims=True) for t in totals], axis=0)
    spread = jnp.concatenate([stacked, jnp.zeros((LANES - 32, LANES), F32)], axis=0)
    cross_ref[...] = dot_nt(jnp.ones((PW, LANES), F32), spread, HIGHEST)
    for copy in outs:
        copy.wait()


def around(value, axis, steps):
    count = lax.axis_size(axis)
    return lax.ppermute(value, axis, [(s, (s + steps) % count) for s in range(count)])


def vmem():
    return pl.BlockSpec(memory_space=pltpu.VMEM)


def hbm():
    return pl.BlockSpec(memory_space=pltpu.HBM)


def smem():
    return pl.BlockSpec(memory_space=pltpu.SMEM)


def exchange(value):
    return lax.all_to_all(value, "pw", split_axis=0, concat_axis=0, tiled=True)


def planes_call(recv, potential, half, coupling, name="planes"):
    return pl.pallas_call(
        planes_kernel,
        name=name,
        out_shape=(
            jax.ShapeDtypeStruct((PW * ROWS, 2 * LANES), BF),
            jax.ShapeDtypeStruct((32, LANES), F32),
        ),
        in_specs=[hbm()] * 9 + [vmem()],
        out_specs=(hbm(), vmem()),
        scratch_shapes=[
            pltpu.VMEM((PW * ROWS, 2 * LANES), BF),
            pltpu.VMEM((DEPTH, GRID, GRID), F32),
        ]
        + [
            pltpu.VMEM(half[k].shape, BF)
            for k in ("spread", "y_table", "mix_in", "mix_out", "x_inverse", "x_forward", "fold")
        ]
        + [
            pltpu.VMEM((PW * ROWS, 2 * LANES), BF),
            pltpu.VMEM((COLS, LANES), F32),
            pltpu.VMEM((COLS, LANES), F32),
            pltpu.VMEM((SPAN * GRID, LANES), F32),
            pltpu.VMEM((SPAN * STEP, LANES), F32),
            pltpu.VMEM((SPAN * STEP, LANES), F32),
            pltpu.VMEM((SPAN * STEP, LANES), F32),
            pltpu.VMEM((SPAN * STEP, LANES), F32),
            pltpu.VMEM((DEPTH * GRID, LANES), F32),
            pltpu.VMEM((DEPTH * GRID, LANES), F32),
            pltpu.VMEM((PW, LOCAL), jnp.int32),
            pltpu.SMEM((PW, LOCAL), jnp.int32),
            pltpu.SemaphoreType.DMA((14,)),
        ],
        compiler_params=pltpu.CompilerParams(vmem_limit_bytes=64 << 20),
        cost_estimate=pl.CostEstimate(
            flops=20_000_000_000, bytes_accessed=4 << 20, transcendentals=0
        ),
    )(
        recv,
        potential,
        half["spread"],
        half["y_table"],
        half["mix_in"],
        half["mix_out"],
        half["x_inverse"],
        half["x_forward"],
        half["fold"],
        coupling,
    )


def two_parts(exact):
    high = np.asarray(exact).astype(jnp.bfloat16).astype(np.float64)
    return jnp.asarray(np.stack([high, exact - high]), BF)


def per_device(orbitals, potential, projectors, coupling, columns):
    tables = build_tables()
    half = {k: jnp.asarray(v, BF) for k, v in tables.items()}
    block = orbitals[0]
    own_columns = columns.reshape(1, LOCAL)
    scale = 1.0 / math.sqrt(COLS * GRID)
    sent, low_orbitals = pl.pallas_call(
        send_kernel,
        name="lines_out",
        out_shape=(
            jax.ShapeDtypeStruct((PW, ROWS, 2 * LANES), BF),
            jax.ShapeDtypeStruct((BANDS, 2, GRID, LOCAL), BF),
        ),
        in_specs=[hbm(), hbm(), vmem(), hbm()],
        out_specs=(hbm(), hbm()),
        scratch_shapes=[
            pltpu.VMEM((BANDS, 2, GRID, LOCAL), F32),
            pltpu.VMEM((PROJ, 2, GRID, LOCAL), F32),
            pltpu.VMEM((2, PW * ROWS, 2 * GRID), BF),
            pltpu.VMEM((PW, ROWS, 2 * LANES), BF),
            pltpu.VMEM((BANDS, 2, GRID, LOCAL), BF),
            pltpu.SemaphoreType.DMA((12,)),
        ],
        compiler_params=pltpu.CompilerParams(vmem_limit_bytes=64 << 20),
    )(block, projectors, own_columns, two_parts(tables["to_planes"]))
    recv = exchange(sent)
    recv, low_orbitals = lax.optimization_barrier((recv, low_orbitals))
    offsets = (-2, -1, 1, 2)
    others = [around(low_orbitals, "band", -offset) for offset in offsets]

    back, mixed = planes_call(recv.reshape(PW * ROWS, 2 * LANES), potential, half, coupling)
    back, others = lax.optimization_barrier((back, others))
    returned = exchange(back.reshape(PW, ROWS, 2 * LANES)).reshape(PW * ROWS, 2 * LANES)

    applied, cross = pl.pallas_call(
        finish_kernel,
        name="lines_in",
        out_shape=(
            jax.ShapeDtypeStruct((BANDS, 2, GRID, LOCAL), F32),
            jax.ShapeDtypeStruct((PW, LANES), F32),
        ),
        in_specs=[hbm()] * 4 + [vmem()] * 2 + [hbm()] * 4,
        out_specs=(hbm(), vmem()),
        scratch_shapes=[
            pltpu.VMEM((PW * ROWS, 2 * LANES), BF),
            pltpu.VMEM((2, 2 * GRID, PW * ROWS), BF),
            pltpu.VMEM((BANDS, 2, GRID, LOCAL), F32),
            pltpu.VMEM((PROJ, 2, GRID, LOCAL), F32),
            pltpu.VMEM((4, BANDS, 2, GRID, LOCAL), BF),
            pltpu.VMEM((2 * GRID, 2 * LANES), F32),
            pltpu.VMEM((BANDS, 2, GRID, LOCAL), F32),
            pltpu.SemaphoreType.DMA((12,)),
        ],
        compiler_params=pltpu.CompilerParams(vmem_limit_bytes=64 << 20),
    )(
        returned,
        two_parts(tables["from_planes"]),
        block,
        projectors,
        mixed,
        own_columns,
        *others,
    )
    every = exchange(cross)
    summed = jnp.sum(every[:, :32], axis=0).reshape(4, 2, BANDS, BANDS)
    source = lax.axis_index("band") + np.asarray(offsets, np.int32)
    inside = (source >= 0) & (source < lax.axis_size("band"))
    cross_terms = jnp.where(inside[:, None, None, None], summed * scale, 0.0)
    return applied[None], cross_terms[None]


def solution(mesh):
    return jax.shard_map(
        per_device,
        mesh=mesh,
        in_specs=(
            P("band", None, None, None, "pw"),
            P("pw", None, None),
            P(None, None, None, "pw"),
            P(),
            P("pw"),
        ),
        out_specs=(P("band", None, None, None, "pw"), P("band", None, None, None, None)),
        check_vma=False,
    )
```

```python
from functools import partial
import math

import jax
import jax.numpy as jnp
import numpy as np
from jax import lax
from jax.experimental import pallas as pl
from jax.experimental.pallas import tpu as pltpu
from jax.sharding import PartitionSpec as P

GRID = 192
BANDS = 2
PROJ = 8
PW = 32
LOCAL = 128
COLS = PW * LOCAL
DEPTH = GRID // PW
ROWS = 16
GROUPS = 4
SPAN = GRID // GROUPS
LANES = 128
WIDTH = LANES // GROUPS
STEP = LANES + 1
OFFSETS = (-2, -1, 1, 2)
BF = jnp.bfloat16
F32 = jnp.float32
HIGHEST = lax.Precision.HIGHEST


def dft_tables():
    index = np.arange(GRID)
    angle = (index[:, None] * index[None, :] % GRID) * (2.0 * math.pi / GRID)
    factor = 1.0 / math.sqrt(GRID)
    return np.cos(angle) * factor, np.sin(angle) * factor


def rounded(exact):
    return np.asarray(exact).astype(jnp.bfloat16).astype(np.float64)


def side_by_side(exact):
    high = rounded(exact)
    return np.concatenate([high, exact - high], axis=1)


def build_tables():
    cos, sin = dft_tables()
    inverse = np.block([[cos, -sin], [sin, cos]])
    forward = np.block([[cos, sin], [-sin, cos]])
    place = np.zeros((PW, ROWS), np.int64) - 1
    for d in range(PW):
        for ri in range(2):
            for zi in range(DEPTH):
                place[d, ri * DEPTH + zi] = ri * GRID + d * DEPTH + zi
    flat = place.reshape(-1)
    to_planes = np.where((flat >= 0)[:, None], inverse[np.maximum(flat, 0)], 0.0)
    from_planes = np.where((flat >= 0)[None, :], forward[:, np.maximum(flat, 0)], 0.0)
    used = BANDS * 2 * DEPTH
    spread = np.zeros((8, 2 * LANES, 2 * LANES))
    for s in range(8):
        for b in range(BANDS):
            for r in range(2 * DEPTH):
                for g in range(GROUPS):
                    spread[s, b * LANES + s * ROWS + r, g * WIDTH + b * 2 * DEPTH + r] = 1.0
        spread[s, s * ROWS + 2 * DEPTH, LANES:] = 1.0
    mix_in = np.zeros((LANES, 2 * LANES))
    mix_out = np.zeros((2 * LANES, LANES))
    fold = np.zeros((2 * ROWS, LANES))
    for g in range(GROUPS):
        for b in range(BANDS):
            for zi in range(DEPTH):
                re = g * WIDTH + b * 2 * DEPTH + zi
                im = re + DEPTH
                for h in range(GROUPS):
                    other = h * WIDTH + b * 2 * DEPTH + zi
                    for part, factor in ((0, 1.0), (LANES, 1j)):
                        turn = 1j ** (g * h % 4) * factor
                        mix_in[re, part + other] = turn.real
                        mix_in[re, part + other + DEPTH] = -turn.imag
                        mix_in[im, part + other] = turn.imag
                        mix_in[im, part + other + DEPTH] = turn.real
                        turn = turn.conjugate()
                        mix_out[part + other, re] = turn.real
                        mix_out[part + other + DEPTH, re] = -turn.imag
                        mix_out[part + other, im] = turn.imag
                        mix_out[part + other + DEPTH, im] = turn.real
                fold[b * ROWS + zi, re] = 1.0
                fold[b * ROWS + DEPTH + zi, im] = 1.0
    balance = 1.6242 / 16.0 * math.sqrt(GRID)
    x_inverse = np.zeros((GROUPS, 2 * SPAN, 4 * SPAN))
    x_forward = np.zeros((GROUPS, 2 * SPAN, 4 * SPAN))
    for g in range(GROUPS):
        c, s = cos[:SPAN, g::GROUPS] / balance, sin[:SPAN, g::GROUPS] / balance
        x_inverse[g] = side_by_side(np.block([[c.T, -s.T], [s.T, c.T]]))
        x_forward[g] = side_by_side(np.block([[c, s], [-s, c]]))
    return dict(
        to_planes=to_planes,
        from_planes=from_planes,
        spread=spread,
        y_table=np.concatenate([cos, sin], axis=0) * balance,
        mix_in=mix_in,
        mix_out=mix_out,
        x_inverse=x_inverse,
        x_forward=x_forward,
        fold=fold,
    )


def dot(a, b, precision=None):
    return lax.dot_general(
        a, b, (((1,), (0,)), ((), ())), precision=precision, preferred_element_type=F32
    )


def dot_nt(a, b, precision=None):
    return lax.dot_general(
        a, b, (((1,), (1,)), ((), ())), precision=precision, preferred_element_type=F32
    )


def wrapped(freqs):
    return jnp.where(freqs >= GRID // 2, freqs - GRID, freqs)


def load(source, target, sem):
    copy = pltpu.make_async_copy(source, target, sem)
    copy.start()
    return copy


def lane_sums(rows):
    count = rows.shape[0]
    total = jnp.sum(rows, axis=1, keepdims=True)
    row = lax.broadcasted_iota(jnp.int32, (count, LANES), 0)
    lane = lax.broadcasted_iota(jnp.int32, (count, LANES), 1)
    return jnp.sum(jnp.where(row == lane, total, 0.0), axis=0, keepdims=True)


def send_kernel(
    block_hbm,
    beta_hbm,
    columns_hbm,
    table_hbm,
    send_hbm,
    low_hbm,
    columns_ref,
    block_ref,
    beta_ref,
    table_ref,
    lines_ref,
    low_ref,
    sems,
):
    block_copy = load(block_hbm, block_ref, sems.at[0])
    columns_copy = load(columns_hbm, columns_ref, sems.at[10])
    table_copy = load(table_hbm, table_ref, sems.at[1])
    beta_copies = [load(beta_hbm.at[j], beta_ref.at[j], sems.at[2 + j]) for j in range(PROJ)]
    block_copy.wait()
    low_ref[...] = block_ref[...].astype(BF)
    low_copy = load(low_ref, low_hbm, sems.at[11])
    wave = jnp.concatenate(
        [jnp.concatenate([block_ref[b, 0], block_ref[b, 1]], axis=0) for b in range(BANDS)], axis=1
    )
    wave_high = wave.astype(BF)
    wave_low = (wave - wave_high.astype(F32)).astype(BF)
    sums = [None] * (BANDS * PROJ * 2)
    for j in range(PROJ):
        beta_copies[j].wait()
        for b in range(BANDS):
            br, bi = beta_ref[j, 0], beta_ref[j, 1]
            wr, wi = block_ref[b, 0], block_ref[b, 1]
            at = (b * PROJ + j) * 2
            sums[at] = jnp.sum(br * wr + bi * wi, axis=0, keepdims=True)
            sums[at + 1] = jnp.sum(br * wi - bi * wr, axis=0, keepdims=True)
    total = lane_sums(jnp.concatenate(sums, axis=0))
    high = total.astype(BF).astype(F32)
    middle = (total - high).astype(BF).astype(F32)
    low = total - high - middle
    columns_copy.wait()
    cols = columns_ref[...]
    col_x = cols // GRID
    first = jnp.concatenate([col_x, cols - col_x * GRID], axis=1).astype(F32)
    other = jnp.concatenate([high, middle, low], axis=0)
    other = jnp.concatenate([other, jnp.zeros((3, LANES), F32)], axis=1)
    meta = jnp.concatenate([jnp.zeros((2 * DEPTH, 2 * LANES), F32), first, other], axis=0)
    table_copy.wait()
    outs = []
    some = PW // 4
    for start in range(0, PW, some):
        part = slice(start * ROWS, (start + some) * ROWS)
        high_table = table_ref[0, part, :]
        lines = dot(high_table, wave_high) + (
            dot(table_ref[1, part, :], wave_high) + dot(high_table, wave_low)
        )
        lines = lines.reshape(some, ROWS, 2 * LANES) + meta[None]
        lines_ref[start : start + some] = lines.astype(BF)
        piece = pl.ds(start, some)
        outs.append(load(lines_ref.at[piece], send_hbm.at[piece], sems.at[12 + start // some]))
    for copy in outs:
        copy.wait()
    low_copy.wait()


def planes_kernel(
    recv_hbm,
    pot_hbm,
    spread_hbm,
    y_hbm,
    mix_in_hbm,
    mix_out_hbm,
    x_inv_hbm,
    x_fwd_hbm,
    fold_hbm,
    coupling_hbm,
    back_hbm,
    mixed_hbm,
    coupling_ref,
    mixed_ref,
    recv_ref,
    pot_ref,
    spread_ref,
    y_ref,
    mix_in_ref,
    mix_out_ref,
    x_inv_ref,
    x_fwd_ref,
    fold_ref,
    back_ref,
    rows_ref,
    mask_ref,
    grid_ref,
    near_ref,
    far_ref,
    near_out_ref,
    far_out_ref,
    near_pot_ref,
    far_pot_ref,
    place_ref,
    index_ref,
    sems,
):
    pairs = (
        (recv_hbm, recv_ref),
        (spread_hbm, spread_ref),
        (y_hbm, y_ref),
        (mix_in_hbm, mix_in_ref),
        (x_inv_hbm, x_inv_ref),
        (x_fwd_hbm, x_fwd_ref),
        (mix_out_hbm, mix_out_ref),
        (fold_hbm, fold_ref),
        (pot_hbm, pot_ref),
    )
    copies = [load(a, b, sems.at[k]) for k, (a, b) in enumerate(pairs)]
    coupling_copy = load(coupling_hbm, coupling_ref, sems.at[14])

    def clear(i, _):
        grid_ref[pl.ds(pl.multiple_of(i * 256, 256), 256), :] = jnp.zeros((256, LANES), F32)
        return 0

    lax.fori_loop(0, SPAN * GRID // 256, clear, 0)
    copies[0].wait()
    lane = lax.broadcasted_iota(jnp.int32, (1, LANES), 1)
    group_start = (lane // WIDTH * SPAN).astype(F32)
    source = lax.broadcasted_iota(jnp.int32, (PW, PW * ROWS), 0)
    entry = lax.broadcasted_iota(jnp.int32, (PW, PW * ROWS), 1)
    pick = (entry == source * ROWS + 2 * DEPTH).astype(F32).astype(BF)
    xy = dot(pick, recv_ref[...])
    x, y = xy[:, :LANES], xy[:, LANES:]
    for g in range(1, GROUPS):
        x = jnp.where(x >= SPAN, x - SPAN, x)
    place_ref[...] = (x * GRID + y).astype(jnp.int32)
    index_copy = load(place_ref, index_ref, sems.at[13])
    copies[1].wait()
    turned = recv_ref[...].astype(F32).T
    entry = lax.broadcasted_iota(jnp.int32, (32, PW * ROWS), 1)
    sums = jnp.where(entry % ROWS > 2 * DEPTH, turned[:32], 0.0)
    sums = jnp.sum(sums, axis=1, keepdims=True) + jnp.zeros((32, LANES), F32)
    row = lax.broadcasted_iota(jnp.int32, (32, 32), 0)
    column = lax.broadcasted_iota(jnp.int32, (32, 32), 1)
    same = (row // (2 * PROJ) == column // (2 * PROJ)) & (row % 2 == column % 2)
    row = lax.broadcasted_iota(jnp.int32, (32, PROJ), 0)
    column = lax.broadcasted_iota(jnp.int32, (32, PROJ), 1)
    widen = (row // 2 % PROJ == column).astype(F32)
    coupling_copy.wait()
    coupling = coupling_ref[...]
    couple = dot_nt(dot(widen, 0.5 * (coupling + coupling.T), HIGHEST), widen, HIGHEST)
    couple = jnp.where(same, couple * (1.0 / math.sqrt(COLS * GRID)), 0.0)
    mixed_ref[...] = dot(couple, sums, HIGHEST)
    mixed_copy = load(mixed_ref, mixed_hbm, sems.at[14])
    turned = turned.astype(BF)
    for s in range(8):
        for g in range(PW // 8):
            left = jnp.concatenate(
                [
                    turned[0:LANES, g * LANES : (g + 1) * LANES],
                    turned[LANES : 2 * LANES, g * LANES : (g + 1) * LANES],
                ],
                axis=1,
            )
            both = dot(left, spread_ref[s])
            start = (g * 8 + s) * LANES
            rows_ref[start : start + LANES, :] = both[:, :LANES]
            offset = both[:, LANES:] - group_start
            mask_ref[start : start + LANES, :] = jnp.where(
                (offset >= 0.0) & (offset < SPAN), 1.0, 0.0
            )

    index_copy.wait()

    def scatter(i, _):
        base = pl.multiple_of(i * LOCAL, LOCAL)
        for u in range(LOCAL):
            place = pl.ds(index_ref[i, u], 1)
            row = pl.ds(base + u, 1)
            pltpu.store(grid_ref.at[place, :], rows_ref[row, :], mask=mask_ref[row, :] > 0.5)
        return 0

    lax.fori_loop(0, PW, scatter, 0)
    for copy in copies[2:]:
        copy.wait()
    for zi in range(DEPTH):
        part = slice(zi * GRID, (zi + 1) * GRID)
        near_pot_ref[part, :] = pot_ref[zi, :, :LANES]
        far_pot_ref[part, :] = jnp.concatenate(
            [pot_ref[zi, :, LANES:], jnp.zeros((GRID, 2 * LANES - GRID), F32)], axis=1
        )

    def along_y_in(i, _):
        base = pl.multiple_of(i * 2 * GRID, 2 * GRID)
        pair = jnp.concatenate(
            [grid_ref[pl.ds(base, GRID), :], grid_ref[pl.ds(base + GRID, GRID), :]], axis=1
        ).astype(BF)
        both = dot(y_ref[...], pair).astype(BF)
        for h in range(2):
            part = jnp.concatenate(
                [
                    both[:GRID, h * LANES : (h + 1) * LANES],
                    both[GRID:, h * LANES : (h + 1) * LANES],
                ],
                axis=1,
            )
            mixed = dot_nt(mix_in_ref[...], part)
            place = pl.ds((2 * i + h) * STEP, LANES)
            near_ref[place, :] = mixed[:, :LANES]
            far_ref[place, :] = jnp.concatenate(
                [mixed[:, LANES:], jnp.zeros((LANES, 2 * LANES - GRID), F32)], axis=1
            )
        return 0

    lax.fori_loop(0, SPAN // 2, along_y_in, 0, unroll=True)

    for zi in range(DEPTH):
        for g in range(GROUPS):
            part = pl.ds(zi * GRID + g, SPAN, stride=GROUPS)
            pot = jnp.concatenate([near_pot_ref[part, :], far_pot_ref[part, :]], axis=1)
            pot = jnp.concatenate([pot, pot], axis=0)
            for b in range(BANDS):
                lane = g * WIDTH + b * 2 * DEPTH + zi
                places = [pl.ds(lane + ri * DEPTH, SPAN, stride=STEP) for ri in range(2)]
                plane = jnp.concatenate(
                    [
                        jnp.concatenate([ref[place, :] for place in places], axis=0)
                        for ref in (near_ref, far_ref)
                    ],
                    axis=1,
                ).astype(BF)
                field = dot(x_inv_ref[g], jnp.concatenate([plane, plane], axis=0))
                field = (field * pot).astype(BF)
                back = dot(x_fwd_ref[g], jnp.concatenate([field, field], axis=0))
                for ri, place in enumerate(places):
                    near_out_ref[place, :] = back[ri * SPAN : (ri + 1) * SPAN, :LANES]
                    far_out_ref[place, :] = back[ri * SPAN : (ri + 1) * SPAN, LANES:]

    def along_y_out(i, _):
        places = [pl.ds((2 * i + h) * STEP, LANES) for h in range(2)]
        pair = jnp.concatenate(
            [
                jnp.concatenate([near_out_ref[place, :] for place in places], axis=0),
                jnp.concatenate([far_out_ref[place, : GRID - LANES] for place in places], axis=0),
            ],
            axis=1,
        ).astype(BF)
        both = dot_nt(y_ref[...], pair).astype(BF)
        base = pl.multiple_of(i * 2 * GRID, 2 * GRID)
        for h in range(2):
            part = jnp.concatenate(
                [
                    both[:GRID, h * LANES : (h + 1) * LANES],
                    both[GRID:, h * LANES : (h + 1) * LANES],
                ],
                axis=1,
            )
            grid_ref[pl.ds(base + h * GRID, GRID), :] = dot(part, mix_out_ref[...])
        return 0

    lax.fori_loop(0, SPAN // 2, along_y_out, 0, unroll=True)

    def gather(i, _):
        base = pl.multiple_of(i * LOCAL, LOCAL)
        for u in range(LOCAL):
            rows_ref[pl.ds(base + u, 1), :] = grid_ref[pl.ds(index_ref[i, u], 1), :]
        return 0

    lax.fori_loop(0, PW, gather, 0)

    outs = []
    outs.append(mixed_copy)
    for d in range(PW):
        part = slice(d * LANES, (d + 1) * LANES)
        kept = (rows_ref[part, :] * mask_ref[part, :]).astype(BF)
        folded = dot_nt(fold_ref[...], kept).astype(BF)
        back_ref[d * ROWS : (d + 1) * ROWS, 0:LANES] = folded[:ROWS]
        back_ref[d * ROWS : (d + 1) * ROWS, LANES:] = folded[ROWS:]
        if d % 8 == 7:
            piece = pl.ds((d - 7) * ROWS, 8 * ROWS)
            outs.append(load(back_ref.at[piece], back_hbm.at[piece], sems.at[9 + d // 8]))
    for copy in outs:
        copy.wait()


def finish_kernel(
    back_hbm,
    table_hbm,
    block_hbm,
    beta_hbm,
    mixed_hbm,
    columns_hbm,
    other_0,
    other_1,
    other_2,
    other_3,
    applied_hbm,
    cross_hbm,
    mixed_ref,
    columns_ref,
    cross_ref,
    back_ref,
    table_ref,
    block_ref,
    beta_ref,
    others_ref,
    local_ref,
    applied_ref,
    sems,
):
    chunk = 48
    steps = range(0, GRID, chunk)
    back_copy = load(back_hbm, back_ref, sems.at[0])
    table_copy = load(table_hbm, table_ref, sems.at[1])
    columns_copy = load(columns_hbm, columns_ref, sems.at[18])
    mixed_copy = load(mixed_hbm, mixed_ref, sems.at[19])

    def load_chunk(k):
        part = pl.ds(k * chunk, chunk)
        return (
            load(block_hbm.at[:, :, part], block_ref.at[:, :, part], sems.at[6 + 2 * k]),
            load(beta_hbm.at[:, :, part], beta_ref.at[:, :, part], sems.at[7 + 2 * k]),
        )

    chunk_copies = [load_chunk(0)]
    other_copies = [
        load(other, others_ref.at[o], sems.at[2 + o])
        for o, other in enumerate((other_0, other_1, other_2, other_3))
    ]
    chunk_copies += [load_chunk(k) for k in range(1, len(steps))]
    band = lax.axis_index("band")
    bands = lax.axis_size("band")
    columns_copy.wait()
    mixed_copy.wait()
    cols = columns_ref[...]
    col_x = cols // GRID
    fx = wrapped(col_x)
    fy = wrapped(cols - col_x * GRID)
    fxy = fx * fx + fy * fy
    back_copy.wait()
    table_copy.wait()
    local_ref[...] = dot(table_ref[0], back_ref[...]) + dot(table_ref[1], back_ref[...])
    totals = [jnp.zeros((8, LANES), F32) for _ in range(32)]
    outs = []
    for k, start in enumerate(steps):
        part = slice(start, start + chunk)
        for copy in chunk_copies[k]:
            copy.wait()
        fz = wrapped(lax.broadcasted_iota(jnp.int32, (chunk, LANES), 0) + start)
        kinetic = (fz * fz + fxy).astype(F32) * (4.0 / (GRID * GRID))
        low = []
        for b in range(BANDS):
            real = local_ref[start : start + chunk, b * LANES : (b + 1) * LANES]
            imag = local_ref[GRID + start : GRID + start + chunk, b * LANES : (b + 1) * LANES]
            real = real + kinetic * block_ref[b, 0, part]
            imag = imag + kinetic * block_ref[b, 1, part]
            for j in range(PROJ):
                at = (b * PROJ + j) * 2
                mr, mi = mixed_ref[at : at + 1, :], mixed_ref[at + 1 : at + 2, :]
                br, bi = beta_ref[j, 0, part], beta_ref[j, 1, part]
                real = real + mr * br - mi * bi
                imag = imag + mr * bi + mi * br
            applied_ref[b, 0, part] = real
            applied_ref[b, 1, part] = imag
            low.append((real.astype(BF).astype(F32), imag.astype(BF).astype(F32)))
        outs.append(
            load(
                applied_ref.at[:, :, pl.ds(start, chunk)],
                applied_hbm.at[:, :, pl.ds(start, chunk)],
                sems.at[14 + k],
            )
        )
        if k == 0:
            for copy in other_copies:
                copy.wait()
        for o in range(4):
            for m in range(BANDS):
                otr = others_ref[o, m, 0, part].astype(F32)
                oti = others_ref[o, m, 1, part].astype(F32)
                for n in range(BANDS):
                    ar, ai = low[n]
                    real = (otr * ar + oti * ai).reshape(chunk // 8, 8, LANES).sum(0)
                    imag = (otr * ai - oti * ar).reshape(chunk // 8, 8, LANES).sum(0)
                    totals[o * 8 + m * 2 + n] += real
                    totals[o * 8 + 4 + m * 2 + n] += imag
    scale = 1.0 / math.sqrt(COLS * GRID)
    rows = []
    for o, offset in enumerate(OFFSETS):
        inside = (band + offset >= 0) & (band + offset < bands)
        factor = jnp.where(inside, scale, 0.0)
        rows += [jnp.sum(t, axis=0, keepdims=True) * factor for t in totals[o * 8 : o * 8 + 8]]
    sums = lane_sums(jnp.concatenate(rows, axis=0))
    cross_ref[...] = jnp.zeros((PW, LANES), F32) + sums
    outs.append(load(cross_ref, cross_hbm, sems.at[18]))
    for copy in outs:
        copy.wait()


def around(value, axis, steps):
    count = lax.axis_size(axis)
    return lax.ppermute(value, axis, [(s, (s + steps) % count) for s in range(count)])


def hbm():
    return pl.BlockSpec(memory_space=pltpu.HBM)


def exchange(value):
    return lax.all_to_all(value, "pw", split_axis=0, concat_axis=0, tiled=True)


def planes_call(recv, potential, half, coupling, name="planes"):
    return pl.pallas_call(
        planes_kernel,
        name=name,
        out_shape=(
            jax.ShapeDtypeStruct((PW * ROWS, 2 * LANES), BF),
            jax.ShapeDtypeStruct((32, LANES), F32),
        ),
        in_specs=[hbm()] * 10,
        out_specs=(hbm(), hbm()),
        scratch_shapes=[
            pltpu.VMEM((PROJ, PROJ), F32),
            pltpu.VMEM((32, LANES), F32),
            pltpu.VMEM((PW * ROWS, 2 * LANES), BF),
            pltpu.VMEM((DEPTH, GRID, GRID), F32),
        ]
        + [
            pltpu.VMEM(half[k].shape, BF)
            for k in ("spread", "y_table", "mix_in", "mix_out", "x_inverse", "x_forward", "fold")
        ]
        + [
            pltpu.VMEM((PW * ROWS, 2 * LANES), BF),
            pltpu.VMEM((COLS, LANES), F32),
            pltpu.VMEM((COLS, LANES), F32),
            pltpu.VMEM((SPAN * GRID, LANES), F32),
            pltpu.VMEM((SPAN * STEP, LANES), F32),
            pltpu.VMEM((SPAN * STEP, LANES), F32),
            pltpu.VMEM((SPAN * STEP, LANES), F32),
            pltpu.VMEM((SPAN * STEP, LANES), F32),
            pltpu.VMEM((DEPTH * GRID, LANES), F32),
            pltpu.VMEM((DEPTH * GRID, LANES), F32),
            pltpu.VMEM((PW, LOCAL), jnp.int32),
            pltpu.SMEM((PW, LOCAL), jnp.int32),
            pltpu.SemaphoreType.DMA((15,)),
        ],
        compiler_params=pltpu.CompilerParams(vmem_limit_bytes=64 << 20),
        cost_estimate=pl.CostEstimate(
            flops=20_000_000_000, bytes_accessed=4 << 20, transcendentals=0
        ),
    )(
        recv,
        potential,
        half["spread"],
        half["y_table"],
        half["mix_in"],
        half["mix_out"],
        half["x_inverse"],
        half["x_forward"],
        half["fold"],
        coupling,
    )


def two_parts(exact):
    high = rounded(exact)
    return jnp.asarray(np.stack([high, exact - high]), BF)


def per_device(orbitals, potential, projectors, coupling, columns):
    tables = build_tables()
    half = {k: jnp.asarray(v, BF) for k, v in tables.items()}
    block = orbitals[0]
    own_columns = columns.reshape(1, LOCAL)
    sent, low_orbitals = pl.pallas_call(
        send_kernel,
        name="lines_out",
        out_shape=(
            jax.ShapeDtypeStruct((PW, ROWS, 2 * LANES), BF),
            jax.ShapeDtypeStruct((BANDS, 2, GRID, LOCAL), BF),
        ),
        in_specs=[hbm()] * 4,
        out_specs=(hbm(), hbm()),
        scratch_shapes=[
            pltpu.VMEM((1, LOCAL), jnp.int32),
            pltpu.VMEM((BANDS, 2, GRID, LOCAL), F32),
            pltpu.VMEM((PROJ, 2, GRID, LOCAL), F32),
            pltpu.VMEM((2, PW * ROWS, 2 * GRID), BF),
            pltpu.VMEM((PW, ROWS, 2 * LANES), BF),
            pltpu.VMEM((BANDS, 2, GRID, LOCAL), BF),
            pltpu.SemaphoreType.DMA((16,)),
        ],
        compiler_params=pltpu.CompilerParams(vmem_limit_bytes=64 << 20),
    )(block, projectors, own_columns, two_parts(tables["to_planes"]))
    recv = exchange(sent)
    recv, low_orbitals = lax.optimization_barrier((recv, low_orbitals))
    others = [around(low_orbitals, "band", -offset) for offset in OFFSETS]

    back, mixed = planes_call(recv.reshape(PW * ROWS, 2 * LANES), potential, half, coupling)
    back, others = lax.optimization_barrier((back, others))
    returned = exchange(back.reshape(PW, ROWS, 2 * LANES)).reshape(PW * ROWS, 2 * LANES)

    applied, cross = pl.pallas_call(
        finish_kernel,
        name="lines_in",
        out_shape=(
            jax.ShapeDtypeStruct((BANDS, 2, GRID, LOCAL), F32),
            jax.ShapeDtypeStruct((PW, LANES), F32),
        ),
        in_specs=[hbm()] * 10,
        out_specs=(hbm(), hbm()),
        scratch_shapes=[
            pltpu.VMEM((32, LANES), F32),
            pltpu.VMEM((1, LOCAL), jnp.int32),
            pltpu.VMEM((PW, LANES), F32),
            pltpu.VMEM((PW * ROWS, 2 * LANES), BF),
            pltpu.VMEM((2, 2 * GRID, PW * ROWS), BF),
            pltpu.VMEM((BANDS, 2, GRID, LOCAL), F32),
            pltpu.VMEM((PROJ, 2, GRID, LOCAL), F32),
            pltpu.VMEM((4, BANDS, 2, GRID, LOCAL), BF),
            pltpu.VMEM((2 * GRID, 2 * LANES), F32),
            pltpu.VMEM((BANDS, 2, GRID, LOCAL), F32),
            pltpu.SemaphoreType.DMA((20,)),
        ],
        compiler_params=pltpu.CompilerParams(vmem_limit_bytes=64 << 20),
    )(
        returned,
        two_parts(tables["from_planes"]),
        block,
        projectors,
        mixed,
        own_columns,
        *others,
    )
    every = exchange(cross)
    cross_terms = jnp.sum(every[:, :32], axis=0).reshape(4, 2, BANDS, BANDS)
    return applied[None], cross_terms[None]


def solution(mesh):
    return jax.shard_map(
        per_device,
        mesh=mesh,
        in_specs=(
            P("band", None, None, None, "pw"),
            P("pw", None, None),
            P(None, None, None, "pw"),
            P(),
            P("pw"),
        ),
        out_specs=(P("band", None, None, None, "pw"), P("band", None, None, None, None)),
        check_vma=False,
    )
```

```python
from functools import partial
import math

import jax
import jax.numpy as jnp
import numpy as np
from jax import lax
from jax.experimental import pallas as pl
from jax.experimental.pallas import tpu as pltpu
from jax.sharding import PartitionSpec as P

GRID = 192
BANDS = 2
PROJ = 8
PW = 32
LOCAL = 128
COLS = PW * LOCAL
DEPTH = GRID // PW
ROWS = 16
GROUPS = 4
SPAN = GRID // GROUPS
LANES = 128
WIDTH = LANES // GROUPS
STEP = LANES + 1
OFFSETS = (-2, -1, 1, 2)
BF = jnp.bfloat16
F32 = jnp.float32
HIGHEST = lax.Precision.HIGHEST


def dft_tables():
    index = np.arange(GRID)
    angle = (index[:, None] * index[None, :] % GRID) * (2.0 * math.pi / GRID)
    factor = 1.0 / math.sqrt(GRID)
    return np.cos(angle) * factor, np.sin(angle) * factor


def rounded(exact):
    return np.asarray(exact).astype(jnp.bfloat16).astype(np.float64)


def side_by_side(exact):
    high = rounded(exact)
    return np.concatenate([high, exact - high], axis=1)


def build_tables():
    cos, sin = dft_tables()
    inverse = np.block([[cos, -sin], [sin, cos]])
    forward = np.block([[cos, sin], [-sin, cos]])
    place = np.zeros((PW, ROWS), np.int64) - 1
    for d in range(PW):
        for ri in range(2):
            for zi in range(DEPTH):
                place[d, ri * DEPTH + zi] = ri * GRID + d * DEPTH + zi
    flat = place.reshape(-1)
    to_planes = np.where((flat >= 0)[:, None], inverse[np.maximum(flat, 0)], 0.0)
    from_planes = np.where((flat >= 0)[None, :], forward[:, np.maximum(flat, 0)], 0.0)
    used = BANDS * 2 * DEPTH
    spread = np.zeros((8, 2 * LANES, 2 * LANES))
    for s in range(8):
        for b in range(BANDS):
            for r in range(2 * DEPTH):
                for g in range(GROUPS):
                    spread[s, b * LANES + s * ROWS + r, g * WIDTH + b * 2 * DEPTH + r] = 1.0
        spread[s, s * ROWS + 2 * DEPTH, LANES:] = 1.0
    mix_in = np.zeros((LANES, 2 * LANES))
    mix_out = np.zeros((2 * LANES, LANES))
    fold = np.zeros((2 * ROWS, LANES))
    for g in range(GROUPS):
        for b in range(BANDS):
            for zi in range(DEPTH):
                re = g * WIDTH + b * 2 * DEPTH + zi
                im = re + DEPTH
                for h in range(GROUPS):
                    other = h * WIDTH + b * 2 * DEPTH + zi
                    for part, factor in ((0, 1.0), (LANES, 1j)):
                        turn = 1j ** (g * h % 4) * factor
                        mix_in[re, part + other] = turn.real
                        mix_in[re, part + other + DEPTH] = -turn.imag
                        mix_in[im, part + other] = turn.imag
                        mix_in[im, part + other + DEPTH] = turn.real
                        turn = turn.conjugate()
                        mix_out[part + other, re] = turn.real
                        mix_out[part + other + DEPTH, re] = -turn.imag
                        mix_out[part + other, im] = turn.imag
                        mix_out[part + other + DEPTH, im] = turn.real
                fold[b * ROWS + zi, re] = 1.0
                fold[b * ROWS + DEPTH + zi, im] = 1.0
    balance = 1.6242 / 16.0 * math.sqrt(GRID)
    x_inverse = np.zeros((GROUPS, 2 * SPAN, 4 * SPAN))
    x_forward = np.zeros((GROUPS, 2 * SPAN, 4 * SPAN))
    for g in range(GROUPS):
        c, s = cos[:SPAN, g::GROUPS] / balance, sin[:SPAN, g::GROUPS] / balance
        x_inverse[g] = side_by_side(np.block([[c.T, -s.T], [s.T, c.T]]))
        x_forward[g] = side_by_side(np.block([[c, s], [-s, c]]))
    return dict(
        to_planes=to_planes,
        from_planes=from_planes,
        spread=spread,
        y_table=np.concatenate([cos, sin], axis=0) * balance,
        mix_in=mix_in,
        mix_out=mix_out,
        x_inverse=x_inverse,
        x_forward=x_forward,
        fold=fold,
    )


def dot(a, b, precision=None):
    return lax.dot_general(
        a, b, (((1,), (0,)), ((), ())), precision=precision, preferred_element_type=F32
    )


def dot_nt(a, b, precision=None):
    return lax.dot_general(
        a, b, (((1,), (1,)), ((), ())), precision=precision, preferred_element_type=F32
    )


def wrapped(freqs):
    return jnp.where(freqs >= GRID // 2, freqs - GRID, freqs)


def load(source, target, sem):
    copy = pltpu.make_async_copy(source, target, sem)
    copy.start()
    return copy


def lane_sums(rows):
    count = rows.shape[0]
    total = jnp.sum(rows, axis=1, keepdims=True)
    row = lax.broadcasted_iota(jnp.int32, (count, LANES), 0)
    lane = lax.broadcasted_iota(jnp.int32, (count, LANES), 1)
    return jnp.sum(jnp.where(row == lane, total, 0.0), axis=0, keepdims=True)


def send_kernel(
    block_hbm,
    beta_hbm,
    columns_hbm,
    table_hbm,
    send_hbm,
    low_hbm,
    columns_ref,
    block_ref,
    beta_ref,
    table_ref,
    lines_ref,
    low_ref,
    sems,
):
    block_copy = load(block_hbm, block_ref, sems.at[0])
    columns_copy = load(columns_hbm, columns_ref, sems.at[10])
    table_copy = load(table_hbm, table_ref, sems.at[1])
    beta_copies = [load(beta_hbm.at[j], beta_ref.at[j], sems.at[2 + j]) for j in range(PROJ)]
    block_copy.wait()
    low_ref[...] = block_ref[...].astype(BF)
    low_copy = load(low_ref, low_hbm, sems.at[11])
    wave = jnp.concatenate(
        [jnp.concatenate([block_ref[b, 0], block_ref[b, 1]], axis=0) for b in range(BANDS)], axis=1
    )
    wave_high = wave.astype(BF)
    wave_low = (wave - wave_high.astype(F32)).astype(BF)
    sums = [None] * (BANDS * PROJ * 2)
    for j in range(PROJ):
        beta_copies[j].wait()
        for b in range(BANDS):
            br, bi = beta_ref[j, 0], beta_ref[j, 1]
            wr, wi = block_ref[b, 0], block_ref[b, 1]
            at = (b * PROJ + j) * 2
            sums[at] = jnp.sum(br * wr + bi * wi, axis=0, keepdims=True)
            sums[at + 1] = jnp.sum(br * wi - bi * wr, axis=0, keepdims=True)
    total = lane_sums(jnp.concatenate(sums, axis=0))
    high = total.astype(BF).astype(F32)
    middle = (total - high).astype(BF).astype(F32)
    low = total - high - middle
    columns_copy.wait()
    cols = columns_ref[...]
    col_x = cols // GRID
    first = jnp.concatenate([col_x, cols - col_x * GRID], axis=1).astype(F32)
    other = jnp.concatenate([high, middle, low], axis=0)
    other = jnp.concatenate([other, jnp.zeros((3, LANES), F32)], axis=1)
    meta = jnp.concatenate([jnp.zeros((2 * DEPTH, 2 * LANES), F32), first, other], axis=0)
    table_copy.wait()
    outs = []
    some = PW // 4
    for start in range(0, PW, some):
        part = slice(start * ROWS, (start + some) * ROWS)
        high_table = table_ref[0, part, :]
        lines = dot(high_table, wave_high) + (
            dot(table_ref[1, part, :], wave_high) + dot(high_table, wave_low)
        )
        lines = lines.reshape(some, ROWS, 2 * LANES) + meta[None]
        lines_ref[start : start + some] = lines.astype(BF)
        piece = pl.ds(start, some)
        outs.append(load(lines_ref.at[piece], send_hbm.at[piece], sems.at[12 + start // some]))
    for copy in outs:
        copy.wait()
    low_copy.wait()


def planes_kernel(
    recv_hbm,
    pot_hbm,
    spread_hbm,
    y_hbm,
    mix_in_hbm,
    mix_out_hbm,
    x_inv_hbm,
    x_fwd_hbm,
    fold_hbm,
    coupling_hbm,
    back_hbm,
    mixed_hbm,
    coupling_ref,
    mixed_ref,
    recv_ref,
    pot_ref,
    spread_ref,
    y_ref,
    mix_in_ref,
    mix_out_ref,
    x_inv_ref,
    x_fwd_ref,
    fold_ref,
    back_ref,
    rows_ref,
    mask_ref,
    grid_ref,
    near_ref,
    far_ref,
    near_out_ref,
    far_out_ref,
    near_pot_ref,
    far_pot_ref,
    place_ref,
    index_ref,
    sems,
):
    pairs = (
        (recv_hbm, recv_ref),
        (spread_hbm, spread_ref),
        (y_hbm, y_ref),
        (mix_in_hbm, mix_in_ref),
        (x_inv_hbm, x_inv_ref),
        (x_fwd_hbm, x_fwd_ref),
        (mix_out_hbm, mix_out_ref),
        (fold_hbm, fold_ref),
        (pot_hbm, pot_ref),
    )
    copies = [load(a, b, sems.at[k]) for k, (a, b) in enumerate(pairs)]
    coupling_copy = load(coupling_hbm, coupling_ref, sems.at[14])

    def clear(i, _):
        grid_ref[pl.ds(pl.multiple_of(i * 256, 256), 256), :] = jnp.zeros((256, LANES), F32)
        return 0

    lax.fori_loop(0, SPAN * GRID // 256, clear, 0)
    copies[0].wait()
    lane = lax.broadcasted_iota(jnp.int32, (1, LANES), 1)
    group_start = (lane // WIDTH * SPAN).astype(F32)
    source = lax.broadcasted_iota(jnp.int32, (PW, PW * ROWS), 0)
    entry = lax.broadcasted_iota(jnp.int32, (PW, PW * ROWS), 1)
    pick = (entry == source * ROWS + 2 * DEPTH).astype(F32).astype(BF)
    xy = dot(pick, recv_ref[...])
    x, y = xy[:, :LANES], xy[:, LANES:]
    for g in range(1, GROUPS):
        x = jnp.where(x >= SPAN, x - SPAN, x)
    place_ref[...] = (x * GRID + y).astype(jnp.int32)
    index_copy = load(place_ref, index_ref, sems.at[13])
    copies[1].wait()
    turned = recv_ref[...].astype(F32).T
    entry = lax.broadcasted_iota(jnp.int32, (32, PW * ROWS), 1)
    sums = jnp.where(entry % ROWS > 2 * DEPTH, turned[:32], 0.0)
    sums = jnp.sum(sums, axis=1, keepdims=True) + jnp.zeros((32, LANES), F32)
    row = lax.broadcasted_iota(jnp.int32, (32, 32), 0)
    column = lax.broadcasted_iota(jnp.int32, (32, 32), 1)
    same = (row // (2 * PROJ) == column // (2 * PROJ)) & (row % 2 == column % 2)
    row = lax.broadcasted_iota(jnp.int32, (32, PROJ), 0)
    column = lax.broadcasted_iota(jnp.int32, (32, PROJ), 1)
    widen = (row // 2 % PROJ == column).astype(F32)
    coupling_copy.wait()
    coupling = coupling_ref[...]
    couple = dot_nt(dot(widen, 0.5 * (coupling + coupling.T), HIGHEST), widen, HIGHEST)
    couple = jnp.where(same, couple * (1.0 / math.sqrt(COLS * GRID)), 0.0)
    mixed_ref[...] = dot(couple, sums, HIGHEST)
    mixed_copy = load(mixed_ref, mixed_hbm, sems.at[14])
    turned = turned.astype(BF)
    for s in range(8):
        for g in range(PW // 8):
            left = jnp.concatenate(
                [
                    turned[0:LANES, g * LANES : (g + 1) * LANES],
                    turned[LANES : 2 * LANES, g * LANES : (g + 1) * LANES],
                ],
                axis=1,
            )
            both = dot(left, spread_ref[s])
            start = (g * 8 + s) * LANES
            rows_ref[start : start + LANES, :] = both[:, :LANES]
            offset = both[:, LANES:] - group_start
            mask_ref[start : start + LANES, :] = jnp.where(
                (offset >= 0.0) & (offset < SPAN), 1.0, 0.0
            )

    index_copy.wait()

    def scatter(i, _):
        base = pl.multiple_of(i * LOCAL, LOCAL)
        for u in range(LOCAL):
            place = pl.ds(index_ref[i, u], 1)
            row = pl.ds(base + u, 1)
            pltpu.store(grid_ref.at[place, :], rows_ref[row, :], mask=mask_ref[row, :] > 0.5)
        return 0

    lax.fori_loop(0, PW, scatter, 0)
    for copy in copies[2:]:
        copy.wait()
    for zi in range(DEPTH):
        part = slice(zi * GRID, (zi + 1) * GRID)
        near_pot_ref[part, :] = pot_ref[zi, :, :LANES]
        far_pot_ref[part, :] = jnp.concatenate(
            [pot_ref[zi, :, LANES:], jnp.zeros((GRID, 2 * LANES - GRID), F32)], axis=1
        )

    def along_y_in(i, _):
        base = pl.multiple_of(i * 2 * GRID, 2 * GRID)
        pair = jnp.concatenate(
            [grid_ref[pl.ds(base, GRID), :], grid_ref[pl.ds(base + GRID, GRID), :]], axis=1
        ).astype(BF)
        both = dot(y_ref[...], pair).astype(BF)
        for h in range(2):
            part = jnp.concatenate(
                [
                    both[:GRID, h * LANES : (h + 1) * LANES],
                    both[GRID:, h * LANES : (h + 1) * LANES],
                ],
                axis=1,
            )
            mixed = dot_nt(mix_in_ref[...], part)
            place = pl.ds((2 * i + h) * STEP, LANES)
            near_ref[place, :] = mixed[:, :LANES]
            far_ref[place, :] = jnp.concatenate(
                [mixed[:, LANES:], jnp.zeros((LANES, 2 * LANES - GRID), F32)], axis=1
            )
        return 0

    lax.fori_loop(0, SPAN // 2, along_y_in, 0, unroll=True)

    for zi in range(DEPTH):
        for g in range(GROUPS):
            part = pl.ds(zi * GRID + g, SPAN, stride=GROUPS)
            pot = jnp.concatenate([near_pot_ref[part, :], far_pot_ref[part, :]], axis=1)
            pot = jnp.concatenate([pot, pot], axis=0)
            for b in range(BANDS):
                lane = g * WIDTH + b * 2 * DEPTH + zi
                places = [pl.ds(lane + ri * DEPTH, SPAN, stride=STEP) for ri in range(2)]
                plane = jnp.concatenate(
                    [
                        jnp.concatenate([ref[place, :] for place in places], axis=0)
                        for ref in (near_ref, far_ref)
                    ],
                    axis=1,
                ).astype(BF)
                field = dot(x_inv_ref[g], jnp.concatenate([plane, plane], axis=0))
                field = (field * pot).astype(BF)
                back = dot(x_fwd_ref[g], jnp.concatenate([field, field], axis=0))
                for ri, place in enumerate(places):
                    near_out_ref[place, :] = back[ri * SPAN : (ri + 1) * SPAN, :LANES]
                    far_out_ref[place, :] = back[ri * SPAN : (ri + 1) * SPAN, LANES:]

    def along_y_out(i, _):
        places = [pl.ds((2 * i + h) * STEP, LANES) for h in range(2)]
        pair = jnp.concatenate(
            [
                jnp.concatenate([near_out_ref[place, :] for place in places], axis=0),
                jnp.concatenate([far_out_ref[place, : GRID - LANES] for place in places], axis=0),
            ],
            axis=1,
        ).astype(BF)
        both = dot_nt(y_ref[...], pair).astype(BF)
        base = pl.multiple_of(i * 2 * GRID, 2 * GRID)
        for h in range(2):
            part = jnp.concatenate(
                [
                    both[:GRID, h * LANES : (h + 1) * LANES],
                    both[GRID:, h * LANES : (h + 1) * LANES],
                ],
                axis=1,
            )
            grid_ref[pl.ds(base + h * GRID, GRID), :] = dot(part, mix_out_ref[...])
        return 0

    lax.fori_loop(0, SPAN // 2, along_y_out, 0, unroll=True)

    def gather(i, _):
        base = pl.multiple_of(i * LOCAL, LOCAL)
        for u in range(LOCAL):
            rows_ref[pl.ds(base + u, 1), :] = grid_ref[pl.ds(index_ref[i, u], 1), :]
        return 0

    lax.fori_loop(0, PW, gather, 0)

    outs = []
    outs.append(mixed_copy)
    for d in range(PW):
        part = slice(d * LANES, (d + 1) * LANES)
        kept = (rows_ref[part, :] * mask_ref[part, :]).astype(BF)
        folded = dot_nt(fold_ref[...], kept).astype(BF)
        back_ref[d * ROWS : (d + 1) * ROWS, 0:LANES] = folded[:ROWS]
        back_ref[d * ROWS : (d + 1) * ROWS, LANES:] = folded[ROWS:]
        if d % 8 == 7:
            piece = pl.ds((d - 7) * ROWS, 8 * ROWS)
            outs.append(load(back_ref.at[piece], back_hbm.at[piece], sems.at[9 + d // 8]))
    for copy in outs:
        copy.wait()


def finish_kernel(
    back_hbm,
    table_hbm,
    block_hbm,
    beta_hbm,
    mixed_hbm,
    columns_hbm,
    other_0,
    other_1,
    other_2,
    other_3,
    applied_hbm,
    cross_hbm,
    mixed_ref,
    columns_ref,
    cross_ref,
    back_ref,
    table_ref,
    block_ref,
    beta_ref,
    others_ref,
    local_ref,
    applied_ref,
    sems,
):
    chunk = 48
    steps = range(0, GRID, chunk)
    back_copy = load(back_hbm, back_ref, sems.at[0])
    table_copy = load(table_hbm, table_ref, sems.at[1])
    columns_copy = load(columns_hbm, columns_ref, sems.at[18])
    mixed_copy = load(mixed_hbm, mixed_ref, sems.at[19])

    def load_chunk(k):
        part = pl.ds(k * chunk, chunk)
        return (
            load(block_hbm.at[:, :, part], block_ref.at[:, :, part], sems.at[6 + 2 * k]),
            load(beta_hbm.at[:, :, part], beta_ref.at[:, :, part], sems.at[7 + 2 * k]),
        )

    chunk_copies = [load_chunk(0)]
    other_copies = [
        load(other, others_ref.at[o], sems.at[2 + o])
        for o, other in enumerate((other_0, other_1, other_2, other_3))
    ]
    chunk_copies += [load_chunk(k) for k in range(1, len(steps))]
    band = lax.axis_index("band")
    bands = lax.axis_size("band")
    columns_copy.wait()
    mixed_copy.wait()
    cols = columns_ref[...]
    col_x = cols // GRID
    fx = wrapped(col_x)
    fy = wrapped(cols - col_x * GRID)
    fxy = fx * fx + fy * fy
    back_copy.wait()
    table_copy.wait()
    local_ref[...] = dot(table_ref[0], back_ref[...]) + dot(table_ref[1], back_ref[...])
    totals = [jnp.zeros((8, LANES), F32) for _ in range(32)]
    outs = []
    for k, start in enumerate(steps):
        part = slice(start, start + chunk)
        for copy in chunk_copies[k]:
            copy.wait()
        fz = wrapped(lax.broadcasted_iota(jnp.int32, (chunk, LANES), 0) + start)
        kinetic = (fz * fz + fxy).astype(F32) * (4.0 / (GRID * GRID))
        low = []
        for b in range(BANDS):
            real = local_ref[start : start + chunk, b * LANES : (b + 1) * LANES]
            imag = local_ref[GRID + start : GRID + start + chunk, b * LANES : (b + 1) * LANES]
            real = real + kinetic * block_ref[b, 0, part]
            imag = imag + kinetic * block_ref[b, 1, part]
            for j in range(PROJ):
                at = (b * PROJ + j) * 2
                mr, mi = mixed_ref[at : at + 1, :], mixed_ref[at + 1 : at + 2, :]
                br, bi = beta_ref[j, 0, part], beta_ref[j, 1, part]
                real = real + mr * br - mi * bi
                imag = imag + mr * bi + mi * br
            applied_ref[b, 0, part] = real
            applied_ref[b, 1, part] = imag
            low.append((real.astype(BF).astype(F32), imag.astype(BF).astype(F32)))
        outs.append(
            load(
                applied_ref.at[:, :, pl.ds(start, chunk)],
                applied_hbm.at[:, :, pl.ds(start, chunk)],
                sems.at[14 + k],
            )
        )
        if k == 0:
            for copy in other_copies:
                copy.wait()
        for o in range(4):
            for m in range(BANDS):
                otr = others_ref[o, m, 0, part].astype(F32)
                oti = others_ref[o, m, 1, part].astype(F32)
                for n in range(BANDS):
                    ar, ai = low[n]
                    real = (otr * ar + oti * ai).reshape(chunk // 8, 8, LANES).sum(0)
                    imag = (otr * ai - oti * ar).reshape(chunk // 8, 8, LANES).sum(0)
                    totals[o * 8 + m * 2 + n] += real
                    totals[o * 8 + 4 + m * 2 + n] += imag
    scale = 1.0 / math.sqrt(COLS * GRID)
    rows = []
    for o, offset in enumerate(OFFSETS):
        inside = (band + offset >= 0) & (band + offset < bands)
        factor = jnp.where(inside, scale, 0.0)
        rows += [jnp.sum(t, axis=0, keepdims=True) * factor for t in totals[o * 8 : o * 8 + 8]]
    sums = lane_sums(jnp.concatenate(rows, axis=0))
    cross_ref[...] = jnp.zeros((PW, LANES), F32) + sums
    outs.append(load(cross_ref, cross_hbm, sems.at[18]))
    for copy in outs:
        copy.wait()


def around(value, axis, steps):
    count = lax.axis_size(axis)
    return lax.ppermute(value, axis, [(s, (s + steps) % count) for s in range(count)])


def hbm():
    return pl.BlockSpec(memory_space=pltpu.HBM)


def exchange(value):
    return lax.all_to_all(value, "pw", split_axis=0, concat_axis=0, tiled=True)


def planes_call(recv, potential, half, coupling, name="planes"):
    return pl.pallas_call(
        planes_kernel,
        name=name,
        out_shape=(
            jax.ShapeDtypeStruct((PW * ROWS, 2 * LANES), BF),
            jax.ShapeDtypeStruct((32, LANES), F32),
        ),
        in_specs=[hbm()] * 10,
        out_specs=(hbm(), hbm()),
        scratch_shapes=[
            pltpu.VMEM((PROJ, PROJ), F32),
            pltpu.VMEM((32, LANES), F32),
            pltpu.VMEM((PW * ROWS, 2 * LANES), BF),
            pltpu.VMEM((DEPTH, GRID, GRID), F32),
        ]
        + [
            pltpu.VMEM(half[k].shape, BF)
            for k in ("spread", "y_table", "mix_in", "mix_out", "x_inverse", "x_forward", "fold")
        ]
        + [
            pltpu.VMEM((PW * ROWS, 2 * LANES), BF),
            pltpu.VMEM((COLS, LANES), F32),
            pltpu.VMEM((COLS, LANES), F32),
            pltpu.VMEM((SPAN * GRID, LANES), F32),
            pltpu.VMEM((SPAN * STEP, LANES), F32),
            pltpu.VMEM((SPAN * STEP, LANES), F32),
            pltpu.VMEM((SPAN * STEP, LANES), F32),
            pltpu.VMEM((SPAN * STEP, LANES), F32),
            pltpu.VMEM((DEPTH * GRID, LANES), F32),
            pltpu.VMEM((DEPTH * GRID, LANES), F32),
            pltpu.VMEM((PW, LOCAL), jnp.int32),
            pltpu.SMEM((PW, LOCAL), jnp.int32),
            pltpu.SemaphoreType.DMA((15,)),
        ],
        compiler_params=pltpu.CompilerParams(vmem_limit_bytes=64 << 20),
        cost_estimate=pl.CostEstimate(
            flops=20_000_000_000, bytes_accessed=4 << 20, transcendentals=0
        ),
    )(
        recv,
        potential,
        half["spread"],
        half["y_table"],
        half["mix_in"],
        half["mix_out"],
        half["x_inverse"],
        half["x_forward"],
        half["fold"],
        coupling,
    )


def two_parts(exact):
    high = rounded(exact)
    return jnp.asarray(np.stack([high, exact - high]), BF)


def per_device(orbitals, potential, projectors, coupling, columns):
    tables = build_tables()
    half = {k: jnp.asarray(v, BF) for k, v in tables.items()}
    block = orbitals[0]
    own_columns = columns.reshape(1, LOCAL)
    sent, low_orbitals = pl.pallas_call(
        send_kernel,
        name="lines_out",
        out_shape=(
            jax.ShapeDtypeStruct((PW, ROWS, 2 * LANES), BF),
            jax.ShapeDtypeStruct((BANDS, 2, GRID, LOCAL), BF),
        ),
        in_specs=[hbm()] * 4,
        out_specs=(hbm(), hbm()),
        scratch_shapes=[
            pltpu.VMEM((1, LOCAL), jnp.int32),
            pltpu.VMEM((BANDS, 2, GRID, LOCAL), F32),
            pltpu.VMEM((PROJ, 2, GRID, LOCAL), F32),
            pltpu.VMEM((2, PW * ROWS, 2 * GRID), BF),
            pltpu.VMEM((PW, ROWS, 2 * LANES), BF),
            pltpu.VMEM((BANDS, 2, GRID, LOCAL), BF),
            pltpu.SemaphoreType.DMA((16,)),
        ],
        compiler_params=pltpu.CompilerParams(vmem_limit_bytes=64 << 20),
    )(block, projectors, own_columns, two_parts(tables["to_planes"]))
    recv = exchange(sent)
    others = [around(low_orbitals, "band", -offset) for offset in OFFSETS]

    back, mixed = planes_call(recv.reshape(PW * ROWS, 2 * LANES), potential, half, coupling)
    back, others = lax.optimization_barrier((back, others))
    returned = exchange(back.reshape(PW, ROWS, 2 * LANES)).reshape(PW * ROWS, 2 * LANES)

    applied, cross = pl.pallas_call(
        finish_kernel,
        name="lines_in",
        out_shape=(
            jax.ShapeDtypeStruct((BANDS, 2, GRID, LOCAL), F32),
            jax.ShapeDtypeStruct((PW, LANES), F32),
        ),
        in_specs=[hbm()] * 10,
        out_specs=(hbm(), hbm()),
        scratch_shapes=[
            pltpu.VMEM((32, LANES), F32),
            pltpu.VMEM((1, LOCAL), jnp.int32),
            pltpu.VMEM((PW, LANES), F32),
            pltpu.VMEM((PW * ROWS, 2 * LANES), BF),
            pltpu.VMEM((2, 2 * GRID, PW * ROWS), BF),
            pltpu.VMEM((BANDS, 2, GRID, LOCAL), F32),
            pltpu.VMEM((PROJ, 2, GRID, LOCAL), F32),
            pltpu.VMEM((4, BANDS, 2, GRID, LOCAL), BF),
            pltpu.VMEM((2 * GRID, 2 * LANES), F32),
            pltpu.VMEM((BANDS, 2, GRID, LOCAL), F32),
            pltpu.SemaphoreType.DMA((20,)),
        ],
        compiler_params=pltpu.CompilerParams(vmem_limit_bytes=64 << 20),
    )(
        returned,
        two_parts(tables["from_planes"]),
        block,
        projectors,
        mixed,
        own_columns,
        *others,
    )
    every = exchange(cross)
    cross_terms = jnp.sum(every[:, :32], axis=0).reshape(4, 2, BANDS, BANDS)
    return applied[None], cross_terms[None]


def solution(mesh):
    return jax.shard_map(
        per_device,
        mesh=mesh,
        in_specs=(
            P("band", None, None, None, "pw"),
            P("pw", None, None),
            P(None, None, None, "pw"),
            P(),
            P("pw"),
        ),
        out_specs=(P("band", None, None, None, "pw"), P("band", None, None, None, None)),
        check_vma=False,
    )
```

```python
from functools import partial
import math

import jax
import jax.numpy as jnp
import numpy as np
from jax import lax
from jax.experimental import pallas as pl
from jax.experimental.pallas import tpu as pltpu
from jax.sharding import PartitionSpec as P

GRID = 192
BANDS = 2
PROJ = 8
PW = 32
LOCAL = 128
COLS = PW * LOCAL
DEPTH = GRID // PW
ROWS = 16
GROUPS = 4
SPAN = GRID // GROUPS
LANES = 128
WIDTH = LANES // GROUPS
STEP = LANES + 1
OFFSETS = (-2, -1, 1, 2)
BF = jnp.bfloat16
F32 = jnp.float32
HIGHEST = lax.Precision.HIGHEST


def dft_tables():
    index = np.arange(GRID)
    angle = (index[:, None] * index[None, :] % GRID) * (2.0 * math.pi / GRID)
    factor = 1.0 / math.sqrt(GRID)
    return np.cos(angle) * factor, np.sin(angle) * factor


def rounded(exact):
    return np.asarray(exact).astype(jnp.bfloat16).astype(np.float64)


def side_by_side(exact):
    high = rounded(exact)
    return np.concatenate([high, exact - high], axis=1)


def build_tables():
    cos, sin = dft_tables()
    inverse = np.block([[cos, -sin], [sin, cos]])
    forward = np.block([[cos, sin], [-sin, cos]])
    place = np.zeros((PW, ROWS), np.int64) - 1
    for d in range(PW):
        for ri in range(2):
            for zi in range(DEPTH):
                place[d, ri * DEPTH + zi] = ri * GRID + d * DEPTH + zi
    flat = place.reshape(-1)
    to_planes = np.where((flat >= 0)[:, None], inverse[np.maximum(flat, 0)], 0.0)
    from_planes = np.where((flat >= 0)[None, :], forward[:, np.maximum(flat, 0)], 0.0)
    used = BANDS * 2 * DEPTH
    spread = np.zeros((8, 2 * LANES, 2 * LANES))
    for s in range(8):
        for b in range(BANDS):
            for r in range(2 * DEPTH):
                for g in range(GROUPS):
                    spread[s, b * LANES + s * ROWS + r, g * WIDTH + b * 2 * DEPTH + r] = 1.0
        spread[s, s * ROWS + 2 * DEPTH, LANES:] = 1.0
    mix_in = np.zeros((LANES, 2 * LANES))
    mix_out = np.zeros((2 * LANES, LANES))
    fold = np.zeros((2 * ROWS, LANES))
    for g in range(GROUPS):
        for b in range(BANDS):
            for zi in range(DEPTH):
                re = g * WIDTH + b * 2 * DEPTH + zi
                im = re + DEPTH
                for h in range(GROUPS):
                    other = h * WIDTH + b * 2 * DEPTH + zi
                    for part, factor in ((0, 1.0), (LANES, 1j)):
                        turn = 1j ** (g * h % 4) * factor
                        mix_in[re, part + other] = turn.real
                        mix_in[re, part + other + DEPTH] = -turn.imag
                        mix_in[im, part + other] = turn.imag
                        mix_in[im, part + other + DEPTH] = turn.real
                        turn = turn.conjugate()
                        mix_out[part + other, re] = turn.real
                        mix_out[part + other + DEPTH, re] = -turn.imag
                        mix_out[part + other, im] = turn.imag
                        mix_out[part + other + DEPTH, im] = turn.real
                fold[b * ROWS + zi, re] = 1.0
                fold[b * ROWS + DEPTH + zi, im] = 1.0
    balance = 1.6242 / 16.0 * math.sqrt(GRID)
    x_inverse = np.zeros((GROUPS, 2 * SPAN, 4 * SPAN))
    x_forward = np.zeros((GROUPS, 2 * SPAN, 4 * SPAN))
    for g in range(GROUPS):
        c, s = cos[:SPAN, g::GROUPS] / balance, sin[:SPAN, g::GROUPS] / balance
        x_inverse[g] = side_by_side(np.block([[c.T, -s.T], [s.T, c.T]]))
        x_forward[g] = side_by_side(np.block([[c, s], [-s, c]]))
    return dict(
        to_planes=to_planes,
        from_planes=from_planes,
        spread=spread,
        y_table=np.concatenate([cos, sin], axis=0) * balance,
        mix_in=mix_in,
        mix_out=mix_out,
        x_inverse=x_inverse,
        x_forward=x_forward,
        fold=fold,
    )


def dot(a, b, precision=None):
    return lax.dot_general(
        a, b, (((1,), (0,)), ((), ())), precision=precision, preferred_element_type=F32
    )


def dot_nt(a, b, precision=None):
    return lax.dot_general(
        a, b, (((1,), (1,)), ((), ())), precision=precision, preferred_element_type=F32
    )


def wrapped(freqs):
    return jnp.where(freqs >= GRID // 2, freqs - GRID, freqs)


def load(source, target, sem):
    copy = pltpu.make_async_copy(source, target, sem)
    copy.start()
    return copy


def lane_sums(rows):
    count = rows.shape[0]
    total = jnp.sum(rows, axis=1, keepdims=True)
    row = lax.broadcasted_iota(jnp.int32, (count, LANES), 0)
    lane = lax.broadcasted_iota(jnp.int32, (count, LANES), 1)
    return jnp.sum(jnp.where(row == lane, total, 0.0), axis=0, keepdims=True)


def send_kernel(
    block_hbm,
    beta_hbm,
    columns_hbm,
    table_hbm,
    send_hbm,
    low_hbm,
    columns_ref,
    block_ref,
    beta_ref,
    table_ref,
    lines_ref,
    low_ref,
    sems,
):
    block_copy = load(block_hbm, block_ref, sems.at[0])
    columns_copy = load(columns_hbm, columns_ref, sems.at[10])
    table_copy = load(table_hbm, table_ref, sems.at[1])
    beta_copies = [load(beta_hbm.at[j], beta_ref.at[j], sems.at[2 + j]) for j in range(PROJ)]
    block_copy.wait()
    low_ref[...] = block_ref[...].astype(BF)
    low_copy = load(low_ref, low_hbm, sems.at[11])
    wave = jnp.concatenate(
        [jnp.concatenate([block_ref[b, 0], block_ref[b, 1]], axis=0) for b in range(BANDS)], axis=1
    )
    wave_high = wave.astype(BF)
    wave_low = (wave - wave_high.astype(F32)).astype(BF)
    sums = [None] * (BANDS * PROJ * 2)
    for j in range(PROJ):
        beta_copies[j].wait()
        for b in range(BANDS):
            br, bi = beta_ref[j, 0], beta_ref[j, 1]
            wr, wi = block_ref[b, 0], block_ref[b, 1]
            at = (b * PROJ + j) * 2
            sums[at] = jnp.sum(br * wr + bi * wi, axis=0, keepdims=True)
            sums[at + 1] = jnp.sum(br * wi - bi * wr, axis=0, keepdims=True)
    total = lane_sums(jnp.concatenate(sums, axis=0))
    high = total.astype(BF).astype(F32)
    middle = (total - high).astype(BF).astype(F32)
    low = total - high - middle
    columns_copy.wait()
    cols = columns_ref[...]
    col_x = cols // GRID
    first = jnp.concatenate([col_x, cols - col_x * GRID], axis=1).astype(F32)
    other = jnp.concatenate([high, middle, low], axis=0)
    other = jnp.concatenate([other, jnp.zeros((3, LANES), F32)], axis=1)
    meta = jnp.concatenate([jnp.zeros((2 * DEPTH, 2 * LANES), F32), first, other], axis=0)
    table_copy.wait()
    outs = []
    some = PW // 4
    for start in range(0, PW, some):
        part = slice(start * ROWS, (start + some) * ROWS)
        high_table = table_ref[0, part, :]
        lines = dot(high_table, wave_high) + (
            dot(table_ref[1, part, :], wave_high) + dot(high_table, wave_low)
        )
        lines = lines.reshape(some, ROWS, 2 * LANES) + meta[None]
        lines_ref[start : start + some] = lines.astype(BF)
        piece = pl.ds(start, some)
        outs.append(load(lines_ref.at[piece], send_hbm.at[piece], sems.at[12 + start // some]))
    for copy in outs:
        copy.wait()
    low_copy.wait()


def planes_kernel(
    recv_hbm,
    pot_hbm,
    spread_hbm,
    y_hbm,
    mix_in_hbm,
    mix_out_hbm,
    x_inv_hbm,
    x_fwd_hbm,
    fold_hbm,
    coupling_hbm,
    back_hbm,
    mixed_hbm,
    coupling_ref,
    mixed_ref,
    recv_ref,
    pot_ref,
    spread_ref,
    y_ref,
    mix_in_ref,
    mix_out_ref,
    x_inv_ref,
    x_fwd_ref,
    fold_ref,
    back_ref,
    rows_ref,
    mask_ref,
    grid_ref,
    near_ref,
    far_ref,
    near_out_ref,
    far_out_ref,
    near_pot_ref,
    far_pot_ref,
    place_ref,
    index_ref,
    sems,
):
    pairs = (
        (recv_hbm, recv_ref),
        (spread_hbm, spread_ref),
        (y_hbm, y_ref),
        (mix_in_hbm, mix_in_ref),
        (x_inv_hbm, x_inv_ref),
        (x_fwd_hbm, x_fwd_ref),
        (mix_out_hbm, mix_out_ref),
        (fold_hbm, fold_ref),
        (pot_hbm, pot_ref),
    )
    copies = [load(a, b, sems.at[k]) for k, (a, b) in enumerate(pairs)]
    coupling_copy = load(coupling_hbm, coupling_ref, sems.at[14])

    def clear(i, _):
        grid_ref[pl.ds(pl.multiple_of(i * 256, 256), 256), :] = jnp.zeros((256, LANES), F32)
        return 0

    lax.fori_loop(0, SPAN * GRID // 256, clear, 0)
    copies[0].wait()
    lane = lax.broadcasted_iota(jnp.int32, (1, LANES), 1)
    group_start = (lane // WIDTH * SPAN).astype(F32)
    source = lax.broadcasted_iota(jnp.int32, (PW, PW * ROWS), 0)
    entry = lax.broadcasted_iota(jnp.int32, (PW, PW * ROWS), 1)
    pick = (entry == source * ROWS + 2 * DEPTH).astype(F32).astype(BF)
    xy = dot(pick, recv_ref[...])
    x, y = xy[:, :LANES], xy[:, LANES:]
    for g in range(1, GROUPS):
        x = jnp.where(x >= SPAN, x - SPAN, x)
    place_ref[...] = (x * GRID + y).astype(jnp.int32)
    index_copy = load(place_ref, index_ref, sems.at[13])
    copies[1].wait()
    turned = recv_ref[...].astype(F32).T
    entry = lax.broadcasted_iota(jnp.int32, (32, PW * ROWS), 1)
    sums = jnp.where(entry % ROWS > 2 * DEPTH, turned[:32], 0.0)
    sums = jnp.sum(sums, axis=1, keepdims=True) + jnp.zeros((32, LANES), F32)
    row = lax.broadcasted_iota(jnp.int32, (32, 32), 0)
    column = lax.broadcasted_iota(jnp.int32, (32, 32), 1)
    same = (row // (2 * PROJ) == column // (2 * PROJ)) & (row % 2 == column % 2)
    row = lax.broadcasted_iota(jnp.int32, (32, PROJ), 0)
    column = lax.broadcasted_iota(jnp.int32, (32, PROJ), 1)
    widen = (row // 2 % PROJ == column).astype(F32)
    coupling_copy.wait()
    coupling = coupling_ref[...]
    couple = dot_nt(dot(widen, 0.5 * (coupling + coupling.T), HIGHEST), widen, HIGHEST)
    couple = jnp.where(same, couple * (1.0 / math.sqrt(COLS * GRID)), 0.0)
    mixed_ref[...] = dot(couple, sums, HIGHEST)
    mixed_copy = load(mixed_ref, mixed_hbm, sems.at[14])
    turned = turned.astype(BF)
    for s in range(8):
        for g in range(PW // 8):
            left = jnp.concatenate(
                [
                    turned[0:LANES, g * LANES : (g + 1) * LANES],
                    turned[LANES : 2 * LANES, g * LANES : (g + 1) * LANES],
                ],
                axis=1,
            )
            both = dot(left, spread_ref[s])
            start = (g * 8 + s) * LANES
            rows_ref[start : start + LANES, :] = both[:, :LANES]
            offset = both[:, LANES:] - group_start
            mask_ref[start : start + LANES, :] = jnp.where(
                (offset >= 0.0) & (offset < SPAN), 1.0, 0.0
            )

    index_copy.wait()

    def scatter(i, _):
        base = pl.multiple_of(i * LOCAL, LOCAL)
        for u in range(LOCAL):
            place = pl.ds(index_ref[i, u], 1)
            row = pl.ds(base + u, 1)
            pltpu.store(grid_ref.at[place, :], rows_ref[row, :], mask=mask_ref[row, :] > 0.5)
        return 0

    lax.fori_loop(0, PW, scatter, 0)
    for copy in copies[2:]:
        copy.wait()
    for zi in range(DEPTH):
        part = slice(zi * GRID, (zi + 1) * GRID)
        near_pot_ref[part, :] = pot_ref[zi, :, :LANES]
        far_pot_ref[part, :] = jnp.concatenate(
            [pot_ref[zi, :, LANES:], jnp.zeros((GRID, 2 * LANES - GRID), F32)], axis=1
        )

    def along_y_in(i, _):
        base = pl.multiple_of(i * 2 * GRID, 2 * GRID)
        pair = jnp.concatenate(
            [grid_ref[pl.ds(base, GRID), :], grid_ref[pl.ds(base + GRID, GRID), :]], axis=1
        ).astype(BF)
        both = dot(y_ref[...], pair).astype(BF)
        for h in range(2):
            part = jnp.concatenate(
                [
                    both[:GRID, h * LANES : (h + 1) * LANES],
                    both[GRID:, h * LANES : (h + 1) * LANES],
                ],
                axis=1,
            )
            mixed = dot_nt(mix_in_ref[...], part)
            place = pl.ds((2 * i + h) * STEP, LANES)
            near_ref[place, :] = mixed[:, :LANES]
            far_ref[place, :] = jnp.concatenate(
                [mixed[:, LANES:], jnp.zeros((LANES, 2 * LANES - GRID), F32)], axis=1
            )
        return 0

    lax.fori_loop(0, SPAN // 2, along_y_in, 0, unroll=True)

    for zi in range(DEPTH):
        for g in range(GROUPS):
            part = pl.ds(zi * GRID + g, SPAN, stride=GROUPS)
            pot = jnp.concatenate([near_pot_ref[part, :], far_pot_ref[part, :]], axis=1)
            pot = jnp.concatenate([pot, pot], axis=0)
            for b in range(BANDS):
                lane = g * WIDTH + b * 2 * DEPTH + zi
                places = [pl.ds(lane + ri * DEPTH, SPAN, stride=STEP) for ri in range(2)]
                plane = jnp.concatenate(
                    [
                        jnp.concatenate([ref[place, :] for place in places], axis=0)
                        for ref in (near_ref, far_ref)
                    ],
                    axis=1,
                ).astype(BF)
                field = dot(x_inv_ref[g], jnp.concatenate([plane, plane], axis=0))
                field = (field * pot).astype(BF)
                back = dot(x_fwd_ref[g], jnp.concatenate([field, field], axis=0))
                for ri, place in enumerate(places):
                    near_out_ref[place, :] = back[ri * SPAN : (ri + 1) * SPAN, :LANES]
                    far_out_ref[place, :] = back[ri * SPAN : (ri + 1) * SPAN, LANES:]

    def along_y_out(i, _):
        places = [pl.ds((2 * i + h) * STEP, LANES) for h in range(2)]
        pair = jnp.concatenate(
            [
                jnp.concatenate([near_out_ref[place, :] for place in places], axis=0),
                jnp.concatenate([far_out_ref[place, : GRID - LANES] for place in places], axis=0),
            ],
            axis=1,
        ).astype(BF)
        both = dot_nt(y_ref[...], pair).astype(BF)
        base = pl.multiple_of(i * 2 * GRID, 2 * GRID)
        for h in range(2):
            part = jnp.concatenate(
                [
                    both[:GRID, h * LANES : (h + 1) * LANES],
                    both[GRID:, h * LANES : (h + 1) * LANES],
                ],
                axis=1,
            )
            grid_ref[pl.ds(base + h * GRID, GRID), :] = dot(part, mix_out_ref[...])
        return 0

    lax.fori_loop(0, SPAN // 2, along_y_out, 0, unroll=True)

    def gather(i, _):
        base = pl.multiple_of(i * LOCAL, LOCAL)
        for u in range(LOCAL):
            rows_ref[pl.ds(base + u, 1), :] = grid_ref[pl.ds(index_ref[i, u], 1), :]
        return 0

    lax.fori_loop(0, PW, gather, 0)

    outs = []
    outs.append(mixed_copy)
    for d in range(PW):
        part = slice(d * LANES, (d + 1) * LANES)
        kept = (rows_ref[part, :] * mask_ref[part, :]).astype(BF)
        folded = dot_nt(fold_ref[...], kept).astype(BF)
        back_ref[d * ROWS : (d + 1) * ROWS, 0:LANES] = folded[:ROWS]
        back_ref[d * ROWS : (d + 1) * ROWS, LANES:] = folded[ROWS:]
        if d % 8 == 7:
            piece = pl.ds((d - 7) * ROWS, 8 * ROWS)
            outs.append(load(back_ref.at[piece], back_hbm.at[piece], sems.at[9 + d // 8]))
    for copy in outs:
        copy.wait()


def finish_kernel(
    back_hbm,
    table_hbm,
    block_hbm,
    beta_hbm,
    mixed_hbm,
    columns_hbm,
    other_0,
    other_1,
    other_2,
    other_3,
    applied_hbm,
    cross_hbm,
    mixed_ref,
    columns_ref,
    cross_ref,
    back_ref,
    table_ref,
    block_ref,
    beta_ref,
    others_ref,
    local_ref,
    applied_ref,
    sems,
):
    chunk = 48
    steps = range(0, GRID, chunk)
    back_copy = load(back_hbm, back_ref, sems.at[0])
    table_copy = load(table_hbm, table_ref, sems.at[1])
    columns_copy = load(columns_hbm, columns_ref, sems.at[18])
    mixed_copy = load(mixed_hbm, mixed_ref, sems.at[19])

    def load_chunk(k):
        part = pl.ds(k * chunk, chunk)
        return (
            load(block_hbm.at[:, :, part], block_ref.at[:, :, part], sems.at[6 + 2 * k]),
            load(beta_hbm.at[:, :, part], beta_ref.at[:, :, part], sems.at[7 + 2 * k]),
        )

    chunk_copies = [load_chunk(0)]
    other_copies = [
        load(other, others_ref.at[o], sems.at[2 + o])
        for o, other in enumerate((other_0, other_1, other_2, other_3))
    ]
    chunk_copies += [load_chunk(k) for k in range(1, len(steps))]
    band = lax.axis_index("band")
    bands = lax.axis_size("band")
    columns_copy.wait()
    mixed_copy.wait()
    cols = columns_ref[...]
    col_x = cols // GRID
    fx = wrapped(col_x)
    fy = wrapped(cols - col_x * GRID)
    fxy = fx * fx + fy * fy
    back_copy.wait()
    table_copy.wait()
    local_ref[...] = dot(table_ref[0], back_ref[...]) + dot(table_ref[1], back_ref[...])
    totals = [jnp.zeros((8, LANES), F32) for _ in range(32)]
    outs = []
    for k, start in enumerate(steps):
        part = slice(start, start + chunk)
        for copy in chunk_copies[k]:
            copy.wait()
        fz = wrapped(lax.broadcasted_iota(jnp.int32, (chunk, LANES), 0) + start)
        kinetic = (fz * fz + fxy).astype(F32) * (4.0 / (GRID * GRID))
        low = []
        for b in range(BANDS):
            real = local_ref[start : start + chunk, b * LANES : (b + 1) * LANES]
            imag = local_ref[GRID + start : GRID + start + chunk, b * LANES : (b + 1) * LANES]
            real = real + kinetic * block_ref[b, 0, part]
            imag = imag + kinetic * block_ref[b, 1, part]
            for j in range(PROJ):
                at = (b * PROJ + j) * 2
                mr, mi = mixed_ref[at : at + 1, :], mixed_ref[at + 1 : at + 2, :]
                br, bi = beta_ref[j, 0, part], beta_ref[j, 1, part]
                real = real + mr * br - mi * bi
                imag = imag + mr * bi + mi * br
            applied_ref[b, 0, part] = real
            applied_ref[b, 1, part] = imag
            low.append((real.astype(BF).astype(F32), imag.astype(BF).astype(F32)))
        outs.append(
            load(
                applied_ref.at[:, :, pl.ds(start, chunk)],
                applied_hbm.at[:, :, pl.ds(start, chunk)],
                sems.at[14 + k],
            )
        )
        if k == 0:
            for copy in other_copies:
                copy.wait()
        for o in range(4):
            for m in range(BANDS):
                otr = others_ref[o, m, 0, part].astype(F32)
                oti = others_ref[o, m, 1, part].astype(F32)
                for n in range(BANDS):
                    ar, ai = low[n]
                    real = (otr * ar + oti * ai).reshape(chunk // 8, 8, LANES).sum(0)
                    imag = (otr * ai - oti * ar).reshape(chunk // 8, 8, LANES).sum(0)
                    totals[o * 8 + m * 2 + n] += real
                    totals[o * 8 + 4 + m * 2 + n] += imag
    scale = 1.0 / math.sqrt(COLS * GRID)
    rows = []
    for o, offset in enumerate(OFFSETS):
        inside = (band + offset >= 0) & (band + offset < bands)
        factor = jnp.where(inside, scale, 0.0)
        rows += [jnp.sum(t, axis=0, keepdims=True) * factor for t in totals[o * 8 : o * 8 + 8]]
    sums = lane_sums(jnp.concatenate(rows, axis=0))
    cross_ref[...] = jnp.zeros((PW, LANES), F32) + sums
    outs.append(load(cross_ref, cross_hbm, sems.at[18]))
    for copy in outs:
        copy.wait()


def around(value, axis, steps):
    count = lax.axis_size(axis)
    return lax.ppermute(value, axis, [(s, (s + steps) % count) for s in range(count)])


def hbm():
    return pl.BlockSpec(memory_space=pltpu.HBM)


def exchange(value):
    return lax.all_to_all(value, "pw", split_axis=0, concat_axis=0, tiled=True)


def planes_call(recv, potential, half, coupling, name="planes"):
    return pl.pallas_call(
        planes_kernel,
        name=name,
        out_shape=(
            jax.ShapeDtypeStruct((PW * ROWS, 2 * LANES), BF),
            jax.ShapeDtypeStruct((32, LANES), F32),
        ),
        in_specs=[hbm()] * 10,
        out_specs=(hbm(), hbm()),
        scratch_shapes=[
            pltpu.VMEM((PROJ, PROJ), F32),
            pltpu.VMEM((32, LANES), F32),
            pltpu.VMEM((PW * ROWS, 2 * LANES), BF),
            pltpu.VMEM((DEPTH, GRID, GRID), F32),
        ]
        + [
            pltpu.VMEM(half[k].shape, BF)
            for k in ("spread", "y_table", "mix_in", "mix_out", "x_inverse", "x_forward", "fold")
        ]
        + [
            pltpu.VMEM((PW * ROWS, 2 * LANES), BF),
            pltpu.VMEM((COLS + 8, LANES), F32),
            pltpu.VMEM((COLS + 8, LANES), F32),
            pltpu.VMEM((SPAN * GRID + 8, LANES), F32),
            pltpu.VMEM(((SPAN + 1) * STEP + 7, LANES), F32),
            pltpu.VMEM(((SPAN + 1) * STEP + 7, LANES), F32),
            pltpu.VMEM(((SPAN + 1) * STEP + 7, LANES), F32),
            pltpu.VMEM(((SPAN + 1) * STEP + 7, LANES), F32),
            pltpu.VMEM((DEPTH * GRID + 8, LANES), F32),
            pltpu.VMEM((DEPTH * GRID + 8, LANES), F32),
            pltpu.VMEM((PW, LOCAL), jnp.int32),
            pltpu.SMEM((PW, LOCAL), jnp.int32),
            pltpu.SemaphoreType.DMA((15,)),
        ],
        compiler_params=pltpu.CompilerParams(vmem_limit_bytes=64 << 20),
        cost_estimate=pl.CostEstimate(
            flops=20_000_000_000, bytes_accessed=4 << 20, transcendentals=0
        ),
    )(
        recv,
        potential,
        half["spread"],
        half["y_table"],
        half["mix_in"],
        half["mix_out"],
        half["x_inverse"],
        half["x_forward"],
        half["fold"],
        coupling,
    )


def two_parts(exact):
    high = rounded(exact)
    return jnp.asarray(np.stack([high, exact - high]), BF)


def per_device(orbitals, potential, projectors, coupling, columns):
    tables = build_tables()
    half = {k: jnp.asarray(v, BF) for k, v in tables.items()}
    block = orbitals[0]
    own_columns = columns.reshape(1, LOCAL)
    sent, low_orbitals = pl.pallas_call(
        send_kernel,
        name="lines_out",
        out_shape=(
            jax.ShapeDtypeStruct((PW, ROWS, 2 * LANES), BF),
            jax.ShapeDtypeStruct((BANDS, 2, GRID, LOCAL), BF),
        ),
        in_specs=[hbm()] * 4,
        out_specs=(hbm(), hbm()),
        scratch_shapes=[
            pltpu.VMEM((1, LOCAL), jnp.int32),
            pltpu.VMEM((BANDS, 2, GRID, LOCAL), F32),
            pltpu.VMEM((PROJ, 2, GRID, LOCAL), F32),
            pltpu.VMEM((2, PW * ROWS, 2 * GRID), BF),
            pltpu.VMEM((PW, ROWS, 2 * LANES), BF),
            pltpu.VMEM((BANDS, 2, GRID, LOCAL), BF),
            pltpu.SemaphoreType.DMA((16,)),
        ],
        compiler_params=pltpu.CompilerParams(vmem_limit_bytes=64 << 20),
    )(block, projectors, own_columns, two_parts(tables["to_planes"]))
    recv = exchange(sent)
    others = [around(low_orbitals, "band", -offset) for offset in OFFSETS]

    back, mixed = planes_call(recv.reshape(PW * ROWS, 2 * LANES), potential, half, coupling)
    back, others = lax.optimization_barrier((back, others))
    returned = exchange(back.reshape(PW, ROWS, 2 * LANES)).reshape(PW * ROWS, 2 * LANES)

    applied, cross = pl.pallas_call(
        finish_kernel,
        name="lines_in",
        out_shape=(
            jax.ShapeDtypeStruct((BANDS, 2, GRID, LOCAL), F32),
            jax.ShapeDtypeStruct((PW, LANES), F32),
        ),
        in_specs=[hbm()] * 10,
        out_specs=(hbm(), hbm()),
        scratch_shapes=[
            pltpu.VMEM((32, LANES), F32),
            pltpu.VMEM((1, LOCAL), jnp.int32),
            pltpu.VMEM((PW, LANES), F32),
            pltpu.VMEM((PW * ROWS, 2 * LANES), BF),
            pltpu.VMEM((2, 2 * GRID, PW * ROWS), BF),
            pltpu.VMEM((BANDS, 2, GRID, LOCAL), F32),
            pltpu.VMEM((PROJ, 2, GRID, LOCAL), F32),
            pltpu.VMEM((4, BANDS, 2, GRID, LOCAL), BF),
            pltpu.VMEM((2 * GRID, 2 * LANES), F32),
            pltpu.VMEM((BANDS, 2, GRID, LOCAL), F32),
            pltpu.SemaphoreType.DMA((20,)),
        ],
        compiler_params=pltpu.CompilerParams(vmem_limit_bytes=64 << 20),
    )(
        returned,
        two_parts(tables["from_planes"]),
        block,
        projectors,
        mixed,
        own_columns,
        *others,
    )
    every = exchange(cross)
    cross_terms = jnp.sum(every[:, :32], axis=0).reshape(4, 2, BANDS, BANDS)
    return applied[None], cross_terms[None]


def solution(mesh):
    return jax.shard_map(
        per_device,
        mesh=mesh,
        in_specs=(
            P("band", None, None, None, "pw"),
            P("pw", None, None),
            P(None, None, None, "pw"),
            P(),
            P("pw"),
        ),
        out_specs=(P("band", None, None, None, "pw"), P("band", None, None, None, None)),
        check_vma=False,
    )
```

```python
from functools import partial
import math

import jax
import jax.numpy as jnp
import numpy as np
from jax import lax
from jax.experimental import pallas as pl
from jax.experimental.pallas import tpu as pltpu
from jax.sharding import PartitionSpec as P

GRID = 192
BANDS = 2
PROJ = 8
PW = 32
LOCAL = 128
COLS = PW * LOCAL
DEPTH = GRID // PW
ROWS = 16
GROUPS = 4
SPAN = GRID // GROUPS
LANES = 128
WIDTH = LANES // GROUPS
STEP = LANES + 1
OFFSETS = (-2, -1, 1, 2)
BF = jnp.bfloat16
F32 = jnp.float32
HIGHEST = lax.Precision.HIGHEST


def dft_tables():
    index = np.arange(GRID)
    angle = (index[:, None] * index[None, :] % GRID) * (2.0 * math.pi / GRID)
    factor = 1.0 / math.sqrt(GRID)
    return np.cos(angle) * factor, np.sin(angle) * factor


def rounded(exact):
    return np.asarray(exact).astype(jnp.bfloat16).astype(np.float64)


def side_by_side(exact):
    high = rounded(exact)
    return np.concatenate([high, exact - high], axis=1)


def build_tables():
    cos, sin = dft_tables()
    inverse = np.block([[cos, -sin], [sin, cos]])
    forward = np.block([[cos, sin], [-sin, cos]])
    place = np.zeros((PW, ROWS), np.int64) - 1
    for d in range(PW):
        for ri in range(2):
            for zi in range(DEPTH):
                place[d, ri * DEPTH + zi] = ri * GRID + d * DEPTH + zi
    flat = place.reshape(-1)
    to_planes = np.where((flat >= 0)[:, None], inverse[np.maximum(flat, 0)], 0.0)
    from_planes = np.where((flat >= 0)[None, :], forward[:, np.maximum(flat, 0)], 0.0)
    used = BANDS * 2 * DEPTH
    spread = np.zeros((8, 2 * LANES, 2 * LANES))
    for s in range(8):
        for b in range(BANDS):
            for r in range(2 * DEPTH):
                for g in range(GROUPS):
                    spread[s, b * LANES + s * ROWS + r, g * WIDTH + b * 2 * DEPTH + r] = 1.0
        spread[s, s * ROWS + 2 * DEPTH, LANES:] = 1.0
    mix_in = np.zeros((LANES, 2 * LANES))
    mix_out = np.zeros((2 * LANES, LANES))
    fold = np.zeros((2 * ROWS, LANES))
    for g in range(GROUPS):
        for b in range(BANDS):
            for zi in range(DEPTH):
                re = g * WIDTH + b * 2 * DEPTH + zi
                im = re + DEPTH
                for h in range(GROUPS):
                    other = h * WIDTH + b * 2 * DEPTH + zi
                    for part, factor in ((0, 1.0), (LANES, 1j)):
                        turn = 1j ** (g * h % 4) * factor
                        mix_in[re, part + other] = turn.real
                        mix_in[re, part + other + DEPTH] = -turn.imag
                        mix_in[im, part + other] = turn.imag
                        mix_in[im, part + other + DEPTH] = turn.real
                        turn = turn.conjugate()
                        mix_out[part + other, re] = turn.real
                        mix_out[part + other + DEPTH, re] = -turn.imag
                        mix_out[part + other, im] = turn.imag
                        mix_out[part + other + DEPTH, im] = turn.real
                fold[b * ROWS + zi, re] = 1.0
                fold[b * ROWS + DEPTH + zi, im] = 1.0
    balance = 1.6242 / 16.0 * math.sqrt(GRID)
    x_inverse = np.zeros((GROUPS, 2 * SPAN, 4 * SPAN))
    x_forward = np.zeros((GROUPS, 2 * SPAN, 4 * SPAN))
    for g in range(GROUPS):
        c, s = cos[:SPAN, g::GROUPS] / balance, sin[:SPAN, g::GROUPS] / balance
        x_inverse[g] = side_by_side(np.block([[c.T, -s.T], [s.T, c.T]]))
        x_forward[g] = side_by_side(np.block([[c, s], [-s, c]]) / balance)
    return dict(
        to_planes=to_planes,
        from_planes=from_planes * balance,
        spread=spread,
        y_table=np.concatenate([cos, sin], axis=0) * balance,
        mix_in=mix_in,
        mix_out=mix_out,
        x_inverse=x_inverse,
        x_forward=x_forward,
        fold=fold,
    )


def dot(a, b, precision=None):
    return lax.dot_general(
        a, b, (((1,), (0,)), ((), ())), precision=precision, preferred_element_type=F32
    )


def dot_nt(a, b, precision=None):
    return lax.dot_general(
        a, b, (((1,), (1,)), ((), ())), precision=precision, preferred_element_type=F32
    )


def wrapped(freqs):
    return jnp.where(freqs >= GRID // 2, freqs - GRID, freqs)


def load(source, target, sem):
    copy = pltpu.make_async_copy(source, target, sem)
    copy.start()
    return copy


def lane_sums(rows):
    count = rows.shape[0]
    total = jnp.sum(rows, axis=1, keepdims=True)
    row = lax.broadcasted_iota(jnp.int32, (count, LANES), 0)
    lane = lax.broadcasted_iota(jnp.int32, (count, LANES), 1)
    return jnp.sum(jnp.where(row == lane, total, 0.0), axis=0, keepdims=True)


def send_kernel(
    block_hbm,
    beta_hbm,
    columns_hbm,
    table_hbm,
    send_hbm,
    low_hbm,
    columns_ref,
    block_ref,
    beta_ref,
    table_ref,
    lines_ref,
    low_ref,
    sems,
):
    block_copy = load(block_hbm, block_ref, sems.at[0])
    columns_copy = load(columns_hbm, columns_ref, sems.at[10])
    table_copy = load(table_hbm, table_ref, sems.at[1])
    beta_copies = [load(beta_hbm.at[j], beta_ref.at[j], sems.at[2 + j]) for j in range(PROJ)]
    block_copy.wait()
    low_ref[...] = block_ref[...].astype(BF)
    low_copy = load(low_ref, low_hbm, sems.at[11])
    wave = jnp.concatenate(
        [jnp.concatenate([block_ref[b, 0], block_ref[b, 1]], axis=0) for b in range(BANDS)], axis=1
    )
    wave_high = wave.astype(BF)
    wave_low = (wave - wave_high.astype(F32)).astype(BF)
    sums = [None] * (BANDS * PROJ * 2)
    for j in range(PROJ):
        beta_copies[j].wait()
        for b in range(BANDS):
            br, bi = beta_ref[j, 0], beta_ref[j, 1]
            wr, wi = block_ref[b, 0], block_ref[b, 1]
            at = (b * PROJ + j) * 2
            sums[at] = jnp.sum(br * wr + bi * wi, axis=0, keepdims=True)
            sums[at + 1] = jnp.sum(br * wi - bi * wr, axis=0, keepdims=True)
    total = lane_sums(jnp.concatenate(sums, axis=0))
    high = total.astype(BF).astype(F32)
    middle = (total - high).astype(BF).astype(F32)
    low = total - high - middle
    columns_copy.wait()
    cols = columns_ref[...]
    col_x = cols // GRID
    first = jnp.concatenate([col_x, cols - col_x * GRID], axis=1).astype(F32)
    other = jnp.concatenate([high, middle, low], axis=0)
    other = jnp.concatenate([other, jnp.zeros((3, LANES), F32)], axis=1)
    meta = jnp.concatenate([jnp.zeros((2 * DEPTH, 2 * LANES), F32), first, other], axis=0)
    table_copy.wait()
    outs = []
    some = PW // 4
    for start in range(0, PW, some):
        part = slice(start * ROWS, (start + some) * ROWS)
        high_table = table_ref[0, part, :]
        lines = dot(high_table, wave_high) + (
            dot(table_ref[1, part, :], wave_high) + dot(high_table, wave_low)
        )
        lines = lines.reshape(some, ROWS, 2 * LANES) + meta[None]
        lines_ref[start : start + some] = lines.astype(BF)
        piece = pl.ds(start, some)
        outs.append(load(lines_ref.at[piece], send_hbm.at[piece], sems.at[12 + start // some]))
    for copy in outs:
        copy.wait()
    low_copy.wait()


def planes_kernel(
    recv_hbm,
    pot_hbm,
    spread_hbm,
    y_hbm,
    mix_in_hbm,
    mix_out_hbm,
    x_inv_hbm,
    x_fwd_hbm,
    fold_hbm,
    coupling_hbm,
    back_hbm,
    mixed_hbm,
    coupling_ref,
    mixed_ref,
    recv_ref,
    pot_ref,
    spread_ref,
    y_ref,
    mix_in_ref,
    mix_out_ref,
    x_inv_ref,
    x_fwd_ref,
    fold_ref,
    back_ref,
    rows_ref,
    mask_ref,
    grid_ref,
    near_ref,
    far_ref,
    near_out_ref,
    far_out_ref,
    near_pot_ref,
    far_pot_ref,
    place_ref,
    index_ref,
    sems,
):
    pairs = (
        (recv_hbm, recv_ref),
        (spread_hbm, spread_ref),
        (y_hbm, y_ref),
        (mix_in_hbm, mix_in_ref),
        (x_inv_hbm, x_inv_ref),
        (x_fwd_hbm, x_fwd_ref),
        (mix_out_hbm, mix_out_ref),
        (fold_hbm, fold_ref),
        (pot_hbm, pot_ref),
    )
    copies = [load(a, b, sems.at[k]) for k, (a, b) in enumerate(pairs)]
    coupling_copy = load(coupling_hbm, coupling_ref, sems.at[14])

    def clear(i, _):
        grid_ref[pl.ds(pl.multiple_of(i * 256, 256), 256), :] = jnp.zeros((256, LANES), F32)
        return 0

    lax.fori_loop(0, SPAN * GRID // 256, clear, 0)
    copies[0].wait()
    lane = lax.broadcasted_iota(jnp.int32, (1, LANES), 1)
    group_start = (lane // WIDTH * SPAN).astype(F32)
    source = lax.broadcasted_iota(jnp.int32, (PW, PW * ROWS), 0)
    entry = lax.broadcasted_iota(jnp.int32, (PW, PW * ROWS), 1)
    pick = (entry == source * ROWS + 2 * DEPTH).astype(F32).astype(BF)
    xy = dot(pick, recv_ref[...])
    x, y = xy[:, :LANES], xy[:, LANES:]
    for g in range(1, GROUPS):
        x = jnp.where(x >= SPAN, x - SPAN, x)
    place_ref[...] = (x * GRID + y).astype(jnp.int32)
    index_copy = load(place_ref, index_ref, sems.at[13])
    copies[1].wait()
    turned = recv_ref[...].astype(F32).T
    entry = lax.broadcasted_iota(jnp.int32, (32, PW * ROWS), 1)
    sums = jnp.where(entry % ROWS > 2 * DEPTH, turned[:32], 0.0)
    sums = jnp.sum(sums, axis=1, keepdims=True) + jnp.zeros((32, LANES), F32)
    row = lax.broadcasted_iota(jnp.int32, (32, 32), 0)
    column = lax.broadcasted_iota(jnp.int32, (32, 32), 1)
    same = (row // (2 * PROJ) == column // (2 * PROJ)) & (row % 2 == column % 2)
    row = lax.broadcasted_iota(jnp.int32, (32, PROJ), 0)
    column = lax.broadcasted_iota(jnp.int32, (32, PROJ), 1)
    widen = (row // 2 % PROJ == column).astype(F32)
    coupling_copy.wait()
    coupling = coupling_ref[...]
    couple = dot_nt(dot(widen, 0.5 * (coupling + coupling.T), HIGHEST), widen, HIGHEST)
    couple = jnp.where(same, couple * (1.0 / math.sqrt(COLS * GRID)), 0.0)
    mixed_ref[...] = dot(couple, sums, HIGHEST)
    mixed_copy = load(mixed_ref, mixed_hbm, sems.at[14])
    turned = turned.astype(BF)
    for s in range(8):
        for g in range(PW // 8):
            left = jnp.concatenate(
                [
                    turned[0:LANES, g * LANES : (g + 1) * LANES],
                    turned[LANES : 2 * LANES, g * LANES : (g + 1) * LANES],
                ],
                axis=1,
            )
            both = dot(left, spread_ref[s])
            start = (g * 8 + s) * LANES
            rows_ref[start : start + LANES, :] = both[:, :LANES]
            offset = both[:, LANES:] - group_start
            mask_ref[start : start + LANES, :] = jnp.where(
                (offset >= 0.0) & (offset < SPAN), 1.0, 0.0
            )

    index_copy.wait()

    def scatter(i, _):
        base = pl.multiple_of(i * LOCAL, LOCAL)
        for u in range(LOCAL):
            place = pl.ds(index_ref[i, u], 1)
            row = pl.ds(base + u, 1)
            pltpu.store(grid_ref.at[place, :], rows_ref[row, :], mask=mask_ref[row, :] > 0.5)
        return 0

    lax.fori_loop(0, PW, scatter, 0)
    for copy in copies[2:]:
        copy.wait()
    for zi in range(DEPTH):
        part = slice(zi * GRID, (zi + 1) * GRID)
        near_pot_ref[part, :] = pot_ref[zi, :, :LANES]
        far_pot_ref[part, :] = jnp.concatenate(
            [pot_ref[zi, :, LANES:], jnp.zeros((GRID, 2 * LANES - GRID), F32)], axis=1
        )

    def along_y_in(i, _):
        base = pl.multiple_of(i * 2 * GRID, 2 * GRID)
        pair = jnp.concatenate(
            [grid_ref[pl.ds(base, GRID), :], grid_ref[pl.ds(base + GRID, GRID), :]], axis=1
        ).astype(BF)
        both = dot(y_ref[...], pair).astype(BF)
        for h in range(2):
            part = jnp.concatenate(
                [
                    both[:GRID, h * LANES : (h + 1) * LANES],
                    both[GRID:, h * LANES : (h + 1) * LANES],
                ],
                axis=1,
            )
            mixed = dot_nt(mix_in_ref[...], part)
            place = pl.ds((2 * i + h) * STEP, LANES)
            near_ref[place, :] = mixed[:, :LANES]
            far_ref[place, :] = jnp.concatenate(
                [mixed[:, LANES:], jnp.zeros((LANES, 2 * LANES - GRID), F32)], axis=1
            )
        return 0

    lax.fori_loop(0, SPAN // 2, along_y_in, 0, unroll=True)

    for zi in range(DEPTH):
        for g in range(GROUPS):
            part = pl.ds(zi * GRID + g, SPAN, stride=GROUPS)
            pot = jnp.concatenate([near_pot_ref[part, :], far_pot_ref[part, :]], axis=1)
            pot = jnp.concatenate([pot, pot], axis=0)
            for b in range(BANDS):
                lane = g * WIDTH + b * 2 * DEPTH + zi
                places = [pl.ds(lane + ri * DEPTH, SPAN, stride=STEP) for ri in range(2)]
                plane = jnp.concatenate(
                    [
                        jnp.concatenate([ref[place, :] for place in places], axis=0)
                        for ref in (near_ref, far_ref)
                    ],
                    axis=1,
                ).astype(BF)
                field = dot(x_inv_ref[g], jnp.concatenate([plane, plane], axis=0))
                field = (field * pot).astype(BF)
                back = dot(x_fwd_ref[g], jnp.concatenate([field, field], axis=0))
                for ri, place in enumerate(places):
                    near_out_ref[place, :] = back[ri * SPAN : (ri + 1) * SPAN, :LANES]
                    far_out_ref[place, :] = back[ri * SPAN : (ri + 1) * SPAN, LANES:]

    def along_y_out(i, _):
        places = [pl.ds((2 * i + h) * STEP, LANES) for h in range(2)]
        pair = jnp.concatenate(
            [
                jnp.concatenate([near_out_ref[place, :] for place in places], axis=0),
                jnp.concatenate([far_out_ref[place, : GRID - LANES] for place in places], axis=0),
            ],
            axis=1,
        ).astype(BF)
        both = dot_nt(y_ref[...], pair).astype(BF)
        base = pl.multiple_of(i * 2 * GRID, 2 * GRID)
        for h in range(2):
            part = jnp.concatenate(
                [
                    both[:GRID, h * LANES : (h + 1) * LANES],
                    both[GRID:, h * LANES : (h + 1) * LANES],
                ],
                axis=1,
            )
            grid_ref[pl.ds(base + h * GRID, GRID), :] = dot(part, mix_out_ref[...])
        return 0

    lax.fori_loop(0, SPAN // 2, along_y_out, 0, unroll=True)

    def gather(i, _):
        base = pl.multiple_of(i * LOCAL, LOCAL)
        for u in range(LOCAL):
            rows_ref[pl.ds(base + u, 1), :] = grid_ref[pl.ds(index_ref[i, u], 1), :]
        return 0

    lax.fori_loop(0, PW, gather, 0)

    outs = []
    outs.append(mixed_copy)
    for d in range(PW):
        part = slice(d * LANES, (d + 1) * LANES)
        kept = (rows_ref[part, :] * mask_ref[part, :]).astype(BF)
        folded = dot_nt(fold_ref[...], kept).astype(BF)
        back_ref[d * ROWS : (d + 1) * ROWS, 0:LANES] = folded[:ROWS]
        back_ref[d * ROWS : (d + 1) * ROWS, LANES:] = folded[ROWS:]
        if d % 8 == 7:
            piece = pl.ds((d - 7) * ROWS, 8 * ROWS)
            outs.append(load(back_ref.at[piece], back_hbm.at[piece], sems.at[9 + d // 8]))
    for copy in outs:
        copy.wait()


def finish_kernel(
    back_hbm,
    table_hbm,
    block_hbm,
    beta_hbm,
    mixed_hbm,
    columns_hbm,
    other_0,
    other_1,
    other_2,
    other_3,
    applied_hbm,
    cross_hbm,
    mixed_ref,
    columns_ref,
    cross_ref,
    back_ref,
    table_ref,
    block_ref,
    beta_ref,
    others_ref,
    local_ref,
    applied_ref,
    sems,
):
    chunk = 48
    steps = range(0, GRID, chunk)
    back_copy = load(back_hbm, back_ref, sems.at[0])
    table_copy = load(table_hbm, table_ref, sems.at[1])
    columns_copy = load(columns_hbm, columns_ref, sems.at[18])
    mixed_copy = load(mixed_hbm, mixed_ref, sems.at[19])

    def load_chunk(k):
        part = pl.ds(k * chunk, chunk)
        return (
            load(block_hbm.at[:, :, part], block_ref.at[:, :, part], sems.at[6 + 2 * k]),
            load(beta_hbm.at[:, :, part], beta_ref.at[:, :, part], sems.at[7 + 2 * k]),
        )

    chunk_copies = [load_chunk(0)]
    other_copies = [
        load(other, others_ref.at[o], sems.at[2 + o])
        for o, other in enumerate((other_0, other_1, other_2, other_3))
    ]
    chunk_copies += [load_chunk(k) for k in range(1, len(steps))]
    band = lax.axis_index("band")
    bands = lax.axis_size("band")
    columns_copy.wait()
    mixed_copy.wait()
    cols = columns_ref[...]
    col_x = cols // GRID
    fx = wrapped(col_x)
    fy = wrapped(cols - col_x * GRID)
    fxy = fx * fx + fy * fy
    back_copy.wait()
    table_copy.wait()
    local_ref[...] = dot(table_ref[...], back_ref[...])
    totals = [jnp.zeros((8, LANES), F32) for _ in range(32)]
    outs = []
    for k, start in enumerate(steps):
        part = slice(start, start + chunk)
        for copy in chunk_copies[k]:
            copy.wait()
        fz = wrapped(lax.broadcasted_iota(jnp.int32, (chunk, LANES), 0) + start)
        kinetic = (fz * fz + fxy).astype(F32) * (4.0 / (GRID * GRID))
        low = []
        for b in range(BANDS):
            real = local_ref[start : start + chunk, b * LANES : (b + 1) * LANES]
            imag = local_ref[GRID + start : GRID + start + chunk, b * LANES : (b + 1) * LANES]
            real = real + kinetic * block_ref[b, 0, part]
            imag = imag + kinetic * block_ref[b, 1, part]
            for j in range(PROJ):
                at = (b * PROJ + j) * 2
                mr, mi = mixed_ref[at : at + 1, :], mixed_ref[at + 1 : at + 2, :]
                br, bi = beta_ref[j, 0, part], beta_ref[j, 1, part]
                real = real + mr * br - mi * bi
                imag = imag + mr * bi + mi * br
            applied_ref[b, 0, part] = real
            applied_ref[b, 1, part] = imag
            low.append((real.astype(BF).astype(F32), imag.astype(BF).astype(F32)))
        outs.append(
            load(
                applied_ref.at[:, :, pl.ds(start, chunk)],
                applied_hbm.at[:, :, pl.ds(start, chunk)],
                sems.at[14 + k],
            )
        )
        if k == 0:
            for copy in other_copies:
                copy.wait()
        for o in range(4):
            for m in range(BANDS):
                otr = others_ref[o, m, 0, part].astype(F32)
                oti = others_ref[o, m, 1, part].astype(F32)
                for n in range(BANDS):
                    ar, ai = low[n]
                    real = (otr * ar + oti * ai).reshape(chunk // 8, 8, LANES).sum(0)
                    imag = (otr * ai - oti * ar).reshape(chunk // 8, 8, LANES).sum(0)
                    totals[o * 8 + m * 2 + n] += real
                    totals[o * 8 + 4 + m * 2 + n] += imag
    scale = 1.0 / math.sqrt(COLS * GRID)
    rows = []
    for o, offset in enumerate(OFFSETS):
        inside = (band + offset >= 0) & (band + offset < bands)
        factor = jnp.where(inside, scale, 0.0)
        rows += [jnp.sum(t, axis=0, keepdims=True) * factor for t in totals[o * 8 : o * 8 + 8]]
    sums = lane_sums(jnp.concatenate(rows, axis=0))
    cross_ref[...] = jnp.zeros((PW, LANES), F32) + sums
    outs.append(load(cross_ref, cross_hbm, sems.at[18]))
    for copy in outs:
        copy.wait()


def around(value, axis, steps):
    count = lax.axis_size(axis)
    return lax.ppermute(value, axis, [(s, (s + steps) % count) for s in range(count)])


def hbm():
    return pl.BlockSpec(memory_space=pltpu.HBM)


def exchange(value):
    return lax.all_to_all(value, "pw", split_axis=0, concat_axis=0, tiled=True)


def planes_call(recv, potential, half, coupling, name="planes"):
    return pl.pallas_call(
        planes_kernel,
        name=name,
        out_shape=(
            jax.ShapeDtypeStruct((PW * ROWS, 2 * LANES), BF),
            jax.ShapeDtypeStruct((32, LANES), F32),
        ),
        in_specs=[hbm()] * 10,
        out_specs=(hbm(), hbm()),
        scratch_shapes=[
            pltpu.VMEM((PROJ, PROJ), F32),
            pltpu.VMEM((32, LANES), F32),
            pltpu.VMEM((PW * ROWS, 2 * LANES), BF),
            pltpu.VMEM((DEPTH, GRID, GRID), F32),
        ]
        + [
            pltpu.VMEM(half[k].shape, BF)
            for k in ("spread", "y_table", "mix_in", "mix_out", "x_inverse", "x_forward", "fold")
        ]
        + [
            pltpu.VMEM((PW * ROWS, 2 * LANES), BF),
            pltpu.VMEM((COLS + 8, LANES), F32),
            pltpu.VMEM((COLS + 8, LANES), F32),
            pltpu.VMEM((SPAN * GRID + 8, LANES), F32),
            pltpu.VMEM(((SPAN + 1) * STEP + 7, LANES), F32),
            pltpu.VMEM(((SPAN + 1) * STEP + 7, LANES), F32),
            pltpu.VMEM(((SPAN + 1) * STEP + 7, LANES), F32),
            pltpu.VMEM(((SPAN + 1) * STEP + 7, LANES), F32),
            pltpu.VMEM((DEPTH * GRID + 8, LANES), F32),
            pltpu.VMEM((DEPTH * GRID + 8, LANES), F32),
            pltpu.VMEM((PW, LOCAL), jnp.int32),
            pltpu.SMEM((PW, LOCAL), jnp.int32),
            pltpu.SemaphoreType.DMA((15,)),
        ],
        compiler_params=pltpu.CompilerParams(vmem_limit_bytes=64 << 20),
        cost_estimate=pl.CostEstimate(
            flops=20_000_000_000, bytes_accessed=4 << 20, transcendentals=0
        ),
    )(
        recv,
        potential,
        half["spread"],
        half["y_table"],
        half["mix_in"],
        half["mix_out"],
        half["x_inverse"],
        half["x_forward"],
        half["fold"],
        coupling,
    )


def two_parts(exact):
    high = rounded(exact)
    return jnp.asarray(np.stack([high, exact - high]), BF)


def per_device(orbitals, potential, projectors, coupling, columns):
    tables = build_tables()
    half = {k: jnp.asarray(v, BF) for k, v in tables.items()}
    block = orbitals[0]
    own_columns = columns.reshape(1, LOCAL)
    sent, low_orbitals = pl.pallas_call(
        send_kernel,
        name="lines_out",
        out_shape=(
            jax.ShapeDtypeStruct((PW, ROWS, 2 * LANES), BF),
            jax.ShapeDtypeStruct((BANDS, 2, GRID, LOCAL), BF),
        ),
        in_specs=[hbm()] * 4,
        out_specs=(hbm(), hbm()),
        scratch_shapes=[
            pltpu.VMEM((1, LOCAL), jnp.int32),
            pltpu.VMEM((BANDS, 2, GRID, LOCAL), F32),
            pltpu.VMEM((PROJ, 2, GRID, LOCAL), F32),
            pltpu.VMEM((2, PW * ROWS, 2 * GRID), BF),
            pltpu.VMEM((PW, ROWS, 2 * LANES), BF),
            pltpu.VMEM((BANDS, 2, GRID, LOCAL), BF),
            pltpu.SemaphoreType.DMA((16,)),
        ],
        compiler_params=pltpu.CompilerParams(vmem_limit_bytes=64 << 20),
    )(block, projectors, own_columns, two_parts(tables["to_planes"]))
    recv = exchange(sent)
    others = [around(low_orbitals, "band", -offset) for offset in OFFSETS]

    back, mixed = planes_call(recv.reshape(PW * ROWS, 2 * LANES), potential, half, coupling)
    order = (1, 0, 2, 3)
    back, *held = lax.optimization_barrier((back, *(others[o] for o in order)))
    others = [held[order.index(o)] for o in range(4)]
    returned = exchange(back.reshape(PW, ROWS, 2 * LANES)).reshape(PW * ROWS, 2 * LANES)

    applied, cross = pl.pallas_call(
        finish_kernel,
        name="lines_in",
        out_shape=(
            jax.ShapeDtypeStruct((BANDS, 2, GRID, LOCAL), F32),
            jax.ShapeDtypeStruct((PW, LANES), F32),
        ),
        in_specs=[hbm()] * 10,
        out_specs=(hbm(), hbm()),
        scratch_shapes=[
            pltpu.VMEM((32, LANES), F32),
            pltpu.VMEM((1, LOCAL), jnp.int32),
            pltpu.VMEM((PW, LANES), F32),
            pltpu.VMEM((PW * ROWS, 2 * LANES), BF),
            pltpu.VMEM((2 * GRID, PW * ROWS), BF),
            pltpu.VMEM((BANDS, 2, GRID, LOCAL), F32),
            pltpu.VMEM((PROJ, 2, GRID, LOCAL), F32),
            pltpu.VMEM((4, BANDS, 2, GRID, LOCAL), BF),
            pltpu.VMEM((2 * GRID, 2 * LANES), F32),
            pltpu.VMEM((BANDS, 2, GRID, LOCAL), F32),
            pltpu.SemaphoreType.DMA((20,)),
        ],
        compiler_params=pltpu.CompilerParams(vmem_limit_bytes=64 << 20),
    )(
        returned,
        half["from_planes"],
        block,
        projectors,
        mixed,
        own_columns,
        *others,
    )
    every = exchange(cross)
    cross_terms = jnp.sum(every[:, :32], axis=0).reshape(4, 2, BANDS, BANDS)
    return applied[None], cross_terms[None]


def solution(mesh):
    return jax.shard_map(
        per_device,
        mesh=mesh,
        in_specs=(
            P("band", None, None, None, "pw"),
            P("pw", None, None),
            P(None, None, None, "pw"),
            P(),
            P("pw"),
        ),
        out_specs=(P("band", None, None, None, "pw"), P("band", None, None, None, None)),
        check_vma=False,
    )
```
